32 devices in a mesh: peer: 4 (over y, x), vocab: 8 (over z, core).
Axes of the slice: x: 2, y: 2, z: 4, core: 2. Of those that a mesh axis runs over, the one named last changes fastest.
Arguments:
- hidden: bfloat16 [4, 512, 4096], P('peer'), may hold values from -200 to 200
- head_weight: bfloat16 [4, 4096, 10240], P('peer', None, 'vocab'), may hold values from -0.484375 to 0.484375
- labels: int32 [512], replicated, may hold values from -100 to 10239, as said below
- segments: int32 [512], replicated, may hold values from 0 to 7, never falling along the last dimension, each value on 1 to 128 neighbouring positions
Outputs:
- grad_hidden: float32 [4, 512, 4096], P('peer', None, 'vocab')
- token_loss: float32 [4, 512], P('peer')
The draws below stay inside these ranges and needn't reach their ends.
Inputs may be any that keep to these rules, and one draw needn't show every extreme that they name: `labels`: exactly 256 tokens carry the ignore label -100; every other label names a vocabulary entry.
All inputs are finite; a program needn't handle non-finite values.
Results may differ from the reference program's by a relative error of at most 0.0009.
The reference program's roundings to bfloat16 on the way count: a program that leaves them out, or rounds other values in their place, can miss the bound.
Values may be sent and summed in bfloat16 or wider, within the bound.
No kernel may reach another device: no remote copies, remote signals or barrier semaphores. Data moves between devices by JAX's collectives and lax.ppermute only.
A program may use at most 128 MiB of HBM per device.

```python
import math
import jax
import jax.numpy as jnp
import numpy as np
from jax import lax

D = 4096
TOK = 512
SEGS = 8
VOCAB = 10240
N_PEER = 4


def one_column(base_key, peer_id, column_id, marked):
    column_key = jax.random.fold_in(jax.random.fold_in(jax.random.fold_in(base_key, 11), peer_id), column_id)
    noise_key, scale_key = jax.random.split(column_key)
    noise = jax.random.truncated_normal(noise_key, -6.0, 6.0, (D,), jnp.float32) * D ** (-0.5)
    spread = jnp.exp(jax.random.uniform(scale_key, (), jnp.float32, math.log(0.5), math.log(5.0)))
    return noise * jnp.where(marked, 5.0, spread)


def chosen_columns(base_key):
    column_key = jax.random.fold_in(base_key, 13)
    first_key, second_key = jax.random.split(column_key)
    aligned = TOK // 16
    first_cols = jax.random.randint(first_key, (N_PEER, aligned), 0, VOCAB)
    second_cols = (first_cols + jax.random.randint(second_key, (N_PEER, aligned), 1, VOCAB)) % VOCAB
    return (first_cols, second_cols)


def draw_head_weight(key, part):
    first_cols, second_cols = chosen_columns(key)
    peer_rows = jnp.arange(N_PEER)[:, None]
    marked = jnp.zeros((N_PEER, VOCAB), bool).at[peer_rows, first_cols].set(True).at[peer_rows, second_cols].set(True)
    inner = jax.vmap(one_column, (None, None, 0, 0), 1)
    table = jax.vmap(inner, (None, 0, None, 0), 0)(key, jnp.arange(N_PEER), jnp.arange(VOCAB), marked)
    return table.astype(jnp.bfloat16)


def draw_hidden(key, part):
    key = jax.random.fold_in(key, 3)
    rows_key, noise_key = jax.random.split(key)
    row_scale = jnp.exp(jax.random.uniform(rows_key, (N_PEER, TOK, 1), jnp.float32, math.log(0.4), math.log(4.0)))
    noise = jax.random.truncated_normal(noise_key, -6.0, 6.0, (N_PEER, TOK, D), jnp.float32) * row_scale
    return noise.astype(jnp.bfloat16)


def draw_labels(key, part):
    key = jax.random.fold_in(key, 5)
    order_key, value_key = jax.random.split(key)
    order = jax.random.permutation(order_key, TOK)
    ignored = jnp.zeros((TOK,), jnp.int32).at[order[:TOK // 2]].set(1)
    values = jax.random.randint(value_key, (TOK,), 0, VOCAB)
    return jnp.where(ignored == 1, -100, values).astype(jnp.int32)


def profile(number_of, total, reach, skew):
    loads = [(1 << 20) // math.isqrt(rank ** skew) + 1 for rank in range(2, number_of + 1)]
    spare, counts = total - reach - (number_of - 1), [1] * (number_of - 1)
    while spare > 0:
        movable = [i for i in range(number_of - 1) if counts[i] < reach]
        whole, left = sum([loads[i] for i in movable]), spare
        for i in movable:
            more = min(reach - counts[i], max(1, left * loads[i] // whole), spare)
            counts[i] = counts[i] + more
            spare = spare - more
    return np.array([reach] + counts)


def uneven_parts(own_key, amount, total, reach, lean):
    if amount == 2:
        one = jax.random.randint(own_key, (), max(1, total - reach), min(reach, total - 1) + 1)
        return jnp.stack([one, total - one])
    lengths = jnp.asarray(profile(amount, total, reach, lean), jnp.int32)
    twos = (amount - 1) // 2
    giver, sink = lengths[1:1 + 2 * twos:2], lengths[2:2 + 2 * twos:2]
    margin = jnp.minimum(giver - 1, reach - sink)
    shifted = jax.random.randint(jax.random.fold_in(own_key, 1), (twos,), 0, 1 << 20) % (margin + 1)
    lengths = lengths.at[1:1 + 2 * twos:2].set(giver - shifted).at[2:2 + 2 * twos:2].set(sink + shifted)
    return lengths[jax.random.permutation(jax.random.fold_in(own_key, 2), amount)]


def setup_inputs(seed: int = 0) -> dict:
    splits = jax.random.split(jax.random.key(seed), 5)
    hidden = draw_hidden(jax.random.fold_in(splits[4], 71), 0)
    head_weight = draw_head_weight(jax.random.fold_in(splits[4], 71), 0)
    labels = draw_labels(jax.random.fold_in(splits[4], 71), 0)
    segments = jnp.searchsorted(jnp.cumsum(uneven_parts(splits[3], SEGS, TOK, TOK // 4, 0)), jnp.arange(TOK), side="right").astype(jnp.int32)
    return {"hidden": hidden, "head_weight": head_weight, "labels": labels, "segments": segments}


def token_terms(peer_tiles, row_peak, exp_total, cross_sum, target, labels, segments, own_peer, peers):
    log_norm = row_peak + jnp.log(exp_total)
    expected = cross_sum / exp_total[:, None, :]
    self_term = jnp.diagonal(expected, axis1=0, axis2=1).T
    divergence = self_term[:, None, :] - expected - log_norm[:, None, :] + log_norm[None, :, :]
    forward_div = lax.dynamic_index_in_dim(divergence, own_peer, 0, False)
    backward_div = lax.dynamic_index_in_dim(divergence, own_peer, 1, False)
    labelled = (labels >= 0).astype(jnp.float32)
    own_norm = lax.dynamic_index_in_dim(log_norm, own_peer, 0, False)
    sym_div = jnp.sum(forward_div + backward_div, axis=0) / (peers - 1)
    token_loss = labelled * (own_norm - target + sym_div)
    member = (segments[:, None] == jnp.arange(SEGS, dtype=jnp.int32)[None, :]).astype(jnp.float32)
    seg_totals = jnp.sum(member * labelled[:, None], axis=0)
    seg_count = jnp.sum(member * seg_totals[None, :], axis=1)
    weight = labelled * labels.shape[0] / (SEGS * jnp.maximum(seg_count, 1.0))
    return log_norm, forward_div, token_loss, weight


def logit_gradient(peer_tiles, log_norm, forward_div, weight, target_mask, own_peer, peers):
    log_probs = peer_tiles - log_norm[:, :, None]
    probs = jnp.exp(log_probs)
    own_probs = lax.dynamic_index_in_dim(probs, own_peer, 0, False)
    own_logp = lax.dynamic_index_in_dim(log_probs, own_peer, 0, False)
    mixed = peers * own_probs - jnp.sum(probs, axis=0)
    spread = peers * own_logp - jnp.sum(log_probs, axis=0) - jnp.sum(forward_div, axis=0)[:, None]
    logit_grad = own_probs - target_mask + (mixed + own_probs * spread) / (peers - 1)
    return (weight[:, None] * logit_grad).astype(jnp.bfloat16)


def reference(hidden, head_weight, labels, segments):
    peers = N_PEER
    peer_tiles = jnp.stack([jnp.dot(hidden[i], head_weight[i], preferred_element_type=jnp.float32).astype(jnp.bfloat16) for i in range(peers)]).astype(jnp.float32)
    row_peak = jnp.max(peer_tiles, axis=2)
    scaled = jnp.exp(peer_tiles - row_peak[:, :, None])
    exp_total = jnp.sum(scaled, axis=2)
    cross_sum = jnp.einsum("itv,jtv->ijt", scaled, peer_tiles, precision=lax.Precision.HIGHEST)
    target_mask = (labels[:, None] == jnp.arange(VOCAB, dtype=jnp.int32)[None, :]).astype(jnp.float32)
    grads = []
    losses = []
    for own_peer in range(peers):
        target = jnp.sum(peer_tiles[own_peer] * target_mask, axis=1)
        log_norm, forward_div, token_loss, weight = token_terms(peer_tiles, row_peak, exp_total, cross_sum, target, labels, segments, own_peer, peers)
        logit_grad = logit_gradient(peer_tiles, log_norm, forward_div, weight, target_mask, own_peer, peers)
        grads.append(lax.dot_general(logit_grad, head_weight[own_peer], (((1,), (1,)), ((), ())), preferred_element_type=jnp.float32))
        losses.append(token_loss)
    return jnp.stack(grads), jnp.stack(losses)
```

```python
import functools
import jax
import jax.numpy as jnp
from jax import lax
from jax.experimental import pallas as pl
from jax.experimental.pallas import tpu as pltpu
from jax.sharding import PartitionSpec as P

SEGS = 8
IGNORED = 256
GROUP = 16
LANES = 128
CODE_ROWS = 16
CODE_STEPS = 64.0
CODE_TOP = 32766.0
VMEM = pltpu.CompilerParams(vmem_limit_bytes=48 * 1024 * 1024)


def lane_ids(rows):
    return lax.broadcasted_iota(jnp.int32, (rows, LANES), 1)


def wanted_rank(row, own, block):
    return (own ^ (row // block)) * block + row % block + 1


def project_kernel(own_ref, lab_ref, seg_ref, hid_ref, w_ref, meta_ref, *rest):
    out_refs, (pick_ref, acc_ref) = rest[:-2], rest[-2:]
    step = pl.program_id(0)
    rows, tokens = pick_ref.shape
    block = out_refs[0].shape[0]

    @pl.when(step == 0)
    def _():
        lab = lab_ref[...]
        seg = seg_ref[...]
        on = lab >= 0
        flags = jnp.broadcast_to(on.astype(jnp.float32), (8, tokens)).astype(jnp.bfloat16)
        src = lax.broadcasted_iota(jnp.int32, (tokens, tokens), 0)
        dst = lax.broadcasted_iota(jnp.int32, (tokens, tokens), 1)
        upto = (src <= dst).astype(jnp.float32).astype(jnp.bfloat16)
        rank = jnp.dot(flags, upto, preferred_element_type=jnp.float32)[0:1, :].astype(jnp.int32)
        rank = jnp.where(on, rank, 0)
        row = lax.broadcasted_iota(jnp.int32, (rows, tokens), 0)
        pick = rank == wanted_rank(row, own_ref[0], block)
        pick_ref[...] = pick.astype(jnp.float32).astype(jnp.bfloat16)
        row = lax.broadcasted_iota(jnp.int32, (block, tokens), 0)
        mine = rank == wanted_rank(row, own_ref[0], block)
        label = jnp.sum(jnp.where(mine, lab, 0).astype(jnp.float32), axis=1, keepdims=True)
        doc = jnp.sum(jnp.where(mine, seg, 0).astype(jnp.float32), axis=1, keepdims=True)
        same = on & (seg.astype(jnp.float32) == doc)
        count = jnp.sum(jnp.where(same, 1.0, 0.0), axis=1, keepdims=True)
        weight = float(tokens) / (SEGS * jnp.maximum(count, 1.0))
        lane = lane_ids(block)
        meta_ref[...] = jnp.where(lane == 0, label, jnp.where(lane == 1, weight, 0.0))
        acc_ref[...] = jnp.zeros_like(acc_ref)

    hid = jnp.dot(pick_ref[...], hid_ref[0], preferred_element_type=jnp.float32)
    acc_ref[...] += jnp.dot(hid.astype(jnp.bfloat16), w_ref[0], preferred_element_type=jnp.float32)

    @pl.when(step == pl.num_programs(0) - 1)
    def _():
        for k, out_ref in enumerate(out_refs):
            out_ref[...] = acc_ref[k * block : (k + 1) * block, :].astype(jnp.bfloat16)


def project(own, labels, segments, hidden, head_weight, peers):
    tokens, depth = hidden.shape[1:]
    width = head_weight.shape[2]
    rows = tokens - IGNORED
    block = rows // peers
    part = 512
    whole = lambda shape: pl.BlockSpec(shape, lambda k: (0,) * len(shape))
    return pl.pallas_call(
        project_kernel,
        grid=(depth // part,),
        in_specs=[
            pl.BlockSpec(memory_space=pltpu.SMEM),
            whole((1, tokens)),
            whole((1, tokens)),
            pl.BlockSpec((1, tokens, part), lambda k: (0, 0, k)),
            pl.BlockSpec((1, part, width), lambda k: (0, k, 0)),
        ],
        out_specs=[whole((block, LANES))] + [whole((block, width))] * peers,
        out_shape=[jax.ShapeDtypeStruct((block, LANES), jnp.float32)]
        + [jax.ShapeDtypeStruct((block, width), jnp.bfloat16)] * peers,
        scratch_shapes=[pltpu.VMEM((rows, tokens), jnp.bfloat16), pltpu.VMEM((rows, width), jnp.float32)],
        compiler_params=VMEM,
        cost_estimate=pl.CostEstimate(
            flops=2 * rows * depth * (width + tokens), bytes_accessed=2 * depth * (width + tokens), transcendentals=0
        ),
        name="project",
    )(own, labels, segments, hidden, head_weight)


def pair_list(peers):
    return [(i, j) for i in range(peers) for j in range(peers) if i != j]


def stat_slots(peers):
    pairs = pair_list(peers)
    return peers, {p: peers + n for n, p in enumerate(pairs)}, peers + len(pairs)


def stats_kernel(base_ref, meta_ref, *refs):
    logit_refs, out_ref = refs[:-1], refs[-1]
    peers = len(logit_refs)
    block, width = logit_refs[0].shape
    _, pair_slot, target_slot = stat_slots(peers)
    span = LANES * GROUP // block
    lane = lane_ids(GROUP)
    sums = jnp.zeros((GROUP, LANES), jnp.float32)
    peaks = jnp.zeros((GROUP, LANES), jnp.float32)
    for g in range(block // GROUP):
        rows = slice(g * GROUP, (g + 1) * GROUP)
        label = meta_ref[rows, 0:1].astype(jnp.int32) - base_ref[0]
        peak = []
        for ref in logit_refs:
            top = ref[rows, 0:LANES].astype(jnp.float32)
            for c in range(LANES, width, LANES):
                top = jnp.maximum(top, ref[rows, c : c + LANES].astype(jnp.float32))
            peak.append(jnp.max(top, axis=1, keepdims=True))
        total = [jnp.zeros((GROUP, LANES), jnp.float32) for _ in range(peers)]
        target = [jnp.zeros((GROUP, LANES), jnp.float32) for _ in range(peers)]
        cross = {p: jnp.zeros((GROUP, LANES), jnp.float32) for p in pair_slot}
        for c in range(0, width, LANES):
            l = [ref[rows, c : c + LANES].astype(jnp.float32) for ref in logit_refs]
            e = [jnp.exp(l[k] - peak[k]) for k in range(peers)]
            hit = (lane + c) == label
            for i in range(peers):
                total[i] += e[i]
                target[i] += jnp.where(hit, l[i], 0.0)
                for j in range(i + 1, peers):
                    gap = l[i] - l[j]
                    cross[i, j] += e[i] * gap
                    cross[j, i] -= e[j] * gap

        def put(slot, vals, top):
            nonlocal sums, peaks
            here = lane == g * span + slot
            sums = jnp.where(here, jnp.sum(vals, axis=1, keepdims=True), sums)
            if top is not None:
                peaks = jnp.where(here, top, peaks)

        for i in range(peers):
            put(i, total[i], peak[i])
            put(target_slot + i, target[i], None)
        for (i, j), slot in pair_slot.items():
            put(slot, cross[i, j], peak[i])
    out_ref[0:GROUP, :] = sums
    out_ref[GROUP : 2 * GROUP, :] = peaks


def stats(base, meta, logits):
    block, width = logits[0].shape
    peers = len(logits)
    return pl.pallas_call(
        stats_kernel,
        in_specs=[pl.BlockSpec(memory_space=pltpu.SMEM)] + [pl.BlockSpec(memory_space=pltpu.VMEM)] * (1 + peers),
        out_shape=jax.ShapeDtypeStruct((2 * GROUP, LANES), jnp.float32),
        compiler_params=VMEM,
        cost_estimate=pl.CostEstimate(
            flops=40 * block * width * peers, bytes_accessed=2 * block * width * peers, transcendentals=block * width * peers
        ),
        name="stats",
    )(base, meta, *logits)


def merged(parts):
    top = parts[0][GROUP:, :]
    for part in parts[1:]:
        top = jnp.maximum(top, part[GROUP:, :])
    total = jnp.zeros_like(top)
    for part in parts:
        total += part[:GROUP, :] * jnp.exp(part[GROUP:, :] - top)
    return total, top


def merge_kernel(*refs):
    total, top = merged([ref[...] for ref in refs[:-1]])
    refs[-1][:GROUP, :] = total
    refs[-1][GROUP:, :] = top


def merge(parts):
    return pl.pallas_call(
        merge_kernel,
        in_specs=[pl.BlockSpec(memory_space=pltpu.VMEM)] * len(parts),
        out_shape=jax.ShapeDtypeStruct(parts[0].shape, jnp.float32),
        name="merge",
    )(*parts)


def grad_kernel(count, base_ref, meta_ref, *refs):
    stat_refs, refs = refs[:count], refs[count:]
    peers = len(refs) // 3
    logit_refs, grad_refs, loss_refs = refs[:peers], refs[peers : 2 * peers], refs[2 * peers :]
    block, width = logit_refs[0].shape
    _, pair_slot, target_slot = stat_slots(peers)
    span = LANES * GROUP // block
    lane = lane_ids(GROUP)
    total, top = merged([ref[...] for ref in stat_refs])
    norm = top + jnp.log(jnp.maximum(total, 1e-37))
    losses = [jnp.zeros((GROUP, LANES), jnp.float32) for _ in range(peers)]
    third = 1.0 / (peers - 1)
    for g in range(block // GROUP):
        rows = slice(g * GROUP, (g + 1) * GROUP)
        at = lambda array, slot: array[:, g * span + slot : g * span + slot + 1]
        label = meta_ref[rows, 0:1].astype(jnp.int32) - base_ref[0]
        weight = meta_ref[rows, 1:2]
        inverse = [1.0 / at(total, i) for i in range(peers)]
        norms = [at(norm, i) for i in range(peers)]
        mean = {p: at(total, slot) * inverse[p[0]] for p, slot in pair_slot.items()}
        shift = []
        for i in range(peers):
            ahead = sum(mean[i, j] for j in range(peers) if j != i)
            back = sum(mean[j, i] for j in range(peers) if j != i)
            loss = norms[i] - at(total, target_slot + i) + (ahead + back) * third
            losses[i] = jnp.where(lane == g * span, loss, losses[i])
            shift.append(1.0 + (peers - ahead) * third)
        for c in range(0, width, LANES):
            l = [ref[rows, c : c + LANES].astype(jnp.float32) for ref in logit_refs]
            p = [jnp.exp(l[k] - norms[k]) for k in range(peers)]
            common = sum(l) * third
            rest = sum(p) * third + jnp.where((lane + c) == label, 1.0, 0.0)
            for i in range(peers):
                grad = p[i] * (shift[i] + (l[i] * (peers * third) - common)) - rest
                grad_refs[i][rows, c : c + LANES] = (weight * grad).astype(jnp.bfloat16)
    for i in range(peers):
        loss_refs[i][...] = losses[i]


def gradients(base, meta, parts, logits):
    block, width = logits[0].shape
    peers = len(logits)
    outs = pl.pallas_call(
        functools.partial(grad_kernel, len(parts)),
        in_specs=[pl.BlockSpec(memory_space=pltpu.SMEM)]
        + [pl.BlockSpec(memory_space=pltpu.VMEM)] * (1 + len(parts) + peers),
        out_shape=[jax.ShapeDtypeStruct((block, width), jnp.bfloat16)] * peers
        + [jax.ShapeDtypeStruct((GROUP, LANES), jnp.float32)] * peers,
        compiler_params=VMEM,
        cost_estimate=pl.CostEstimate(
            flops=20 * block * width * peers, bytes_accessed=4 * block * width * peers, transcendentals=block * width * peers
        ),
        name="gradients",
    )(base, meta, *parts, *logits)
    return outs[:peers], outs[peers:]


def share_kernel(order_ref, *refs):
    w_ref, out_ref, all_ref = refs[-3:]
    block = refs[0].shape[0]

    @pl.when(pl.program_id(0) == 0)
    def _():
        for k, ref in enumerate(refs[:-3]):
            all_ref[k * block : (k + 1) * block, :] = ref[...]

    out_ref[0] = lax.dot_general(
        w_ref[0], all_ref[...], (((1,), (1,)), ((), ())), preferred_element_type=jnp.float32
    )


def share(order, grads, head_weight, depth):
    block, width = grads[0].shape
    rows = block * len(grads)
    count = order.shape[0]
    return pl.pallas_call(
        share_kernel,
        grid_spec=pltpu.PrefetchScalarGridSpec(
            num_scalar_prefetch=1,
            grid=(count,),
            in_specs=[pl.BlockSpec((block, width), lambda n, order: (0, 0))] * len(grads)
            + [pl.BlockSpec((1, depth, width), lambda n, order: (0, order[n], 0))],
            out_specs=pl.BlockSpec((1, depth, rows), lambda n, order: (n, 0, 0)),
            scratch_shapes=[pltpu.VMEM((rows, width), jnp.bfloat16)],
        ),
        out_shape=jax.ShapeDtypeStruct((count, depth, rows), jnp.float32),
        compiler_params=VMEM,
        cost_estimate=pl.CostEstimate(
            flops=2 * rows * width * depth * count, bytes_accessed=2 * width * depth * count, transcendentals=0
        ),
        name="share",
    )(order, *grads, head_weight)


def encode_kernel(a_ref, b_ref, out_ref):
    value = a_ref[0] + b_ref[0]
    depth = value.shape[0]
    top = jnp.maximum(jnp.max(jnp.abs(value), axis=0, keepdims=True), 1e-30)
    code = jnp.ceil(jnp.log2(top) * CODE_STEPS)
    unit = jnp.exp2(code * (-1.0 / CODE_STEPS)) * CODE_TOP
    coded = jnp.clip(jnp.round(value * unit), -CODE_TOP - 1, CODE_TOP + 1)
    out_ref[:depth, :] = coded.astype(jnp.int32).astype(jnp.int16)
    codes = jnp.broadcast_to(code, (CODE_ROWS, value.shape[1]))
    out_ref[depth:, :] = codes.astype(jnp.int32).astype(jnp.int16)


def encode(a, b, index):
    _, depth, rows = a.shape
    spec = pl.BlockSpec((1, depth, rows), lambda _: (index, 0, 0))
    return pl.pallas_call(
        encode_kernel,
        grid=(1,),
        in_specs=[spec, spec],
        out_specs=pl.BlockSpec((depth + CODE_ROWS, rows), lambda _: (0, 0)),
        out_shape=jax.ShapeDtypeStruct((depth + CODE_ROWS, rows), jnp.int16),
        compiler_params=VMEM,
        cost_estimate=pl.CostEstimate(flops=8 * depth * rows, bytes_accessed=10 * depth * rows, transcendentals=0),
        name="encode",
    )(a, b)


def finish_kernel(peers, own_ref, row_ref, col_ref, a_ref, b_ref, *refs):
    loss_refs, refs = refs[:peers], refs[peers:]
    coded_refs, (out_ref, loss_ref) = refs[:-2], refs[-2:]
    depth, rows = a_ref.shape[1:]
    tokens = row_ref.shape[1]
    block = rows // peers
    value = a_ref[0] + b_ref[0]
    for ref in coded_refs:
        code = ref[depth : depth + CODE_ROWS, :].astype(jnp.int32).astype(jnp.float32)[0:1, :]
        unit = jnp.exp2(code * (1.0 / CODE_STEPS)) * (1.0 / CODE_TOP)
        value += ref[:depth, :].astype(jnp.int32).astype(jnp.float32) * unit

    src = lax.broadcasted_iota(jnp.int32, (tokens, tokens), 0)
    dst = lax.broadcasted_iota(jnp.int32, (tokens, tokens), 1)
    on = row_ref[...] >= 0
    flags = jnp.broadcast_to(on.astype(jnp.float32), (8, tokens)).astype(jnp.bfloat16)
    upto = (src <= dst).astype(jnp.float32).astype(jnp.bfloat16)
    rank = jnp.dot(flags, upto, preferred_element_type=jnp.float32)[0:1, :].astype(jnp.int32)
    rank = jnp.where(on, rank, 0)
    losses = jnp.zeros((1, tokens), jnp.float32)
    span = LANES * GROUP // block
    for k in range(peers):
        for g in range(block // GROUP):
            row = lax.broadcasted_iota(jnp.int32, (GROUP, tokens), 0) + (k * block + g * GROUP)
            here = rank == wanted_rank(row, own_ref[0], block)
            piece = loss_refs[k][:, g * span : g * span + 1]
            losses += jnp.sum(jnp.where(here, piece, 0.0), axis=0, keepdims=True)
    loss_ref[...] = losses

    on = col_ref[...] >= 0
    flags = jnp.broadcast_to(on.astype(jnp.float32), (tokens, LANES)).astype(jnp.bfloat16)
    upto = (dst <= src).astype(jnp.float32).astype(jnp.bfloat16)
    rank = jnp.dot(upto, flags, preferred_element_type=jnp.float32)[:, 0:1].astype(jnp.int32)
    rank = jnp.where(on, rank, 0)
    row = lax.broadcasted_iota(jnp.int32, (tokens, rows), 1)
    place = (rank == wanted_rank(row, own_ref[0], block)).astype(jnp.float32).astype(jnp.bfloat16)
    result = jnp.zeros((tokens, depth), jnp.float32)
    for _ in range(3):
        piece = value.astype(jnp.bfloat16)
        value = value - piece.astype(jnp.float32)
        result += lax.dot_general(place, piece, (((1,), (1,)), ((), ())), preferred_element_type=jnp.float32)
    out_ref[0] = result


def finish(own, labels, a, b, losses, coded):
    _, depth, rows = a.shape
    tokens = labels.shape[0]
    first = pl.BlockSpec((1, depth, rows), lambda _: (0, 0, 0))
    whole = lambda shape: pl.BlockSpec(shape, lambda _: (0,) * len(shape))
    return pl.pallas_call(
        functools.partial(finish_kernel, len(losses)),
        grid=(1,),
        in_specs=[pl.BlockSpec(memory_space=pltpu.SMEM), whole((1, tokens)), whole((tokens, 1)), first, first]
        + [whole((GROUP, LANES))] * len(losses)
        + [whole((depth + CODE_ROWS, rows))] * len(coded),
        out_specs=[whole((1, tokens, depth)), whole((1, tokens))],
        out_shape=[
            jax.ShapeDtypeStruct((1, tokens, depth), jnp.float32),
            jax.ShapeDtypeStruct((1, tokens), jnp.float32),
        ],
        compiler_params=VMEM,
        cost_estimate=pl.CostEstimate(
            flops=6 * tokens * depth * rows, bytes_accessed=4 * tokens * depth, transcendentals=0
        ),
        name="finish",
    )(own, labels[None, :], labels[:, None], a, b, *losses, *coded)


def swap(array, axis, size, mask):
    return lax.ppermute(array, axis, [(i, i ^ mask) for i in range(size)])


def on_device(hidden, head_weight, labels, segments):
    peers = lax.axis_size("peer")
    shards = lax.axis_size("vocab")
    width = head_weight.shape[2]
    own = lax.axis_index("peer").astype(jnp.int32)
    shard = lax.axis_index("vocab").astype(jnp.int32)
    own_arr = own.reshape(1)
    base = (shard * width).reshape(1)
    depth = head_weight.shape[1] // shards
    chips = [2 * c for c in range(1, shards // 2)]

    meta, *blocks = project(own_arr, labels[None, :], segments[None, :], hidden, head_weight, peers)
    logits = [blocks[0]] + [swap(blocks[k], "peer", peers, k) for k in range(1, peers)]

    part = stats(base, meta, logits)
    part = merge([part, swap(part, "vocab", shards, 1)])
    parts = [part] + [swap(part, "vocab", shards, mask) for mask in chips]
    grads, losses = gradients(base, meta, parts, logits)
    grads = [grads[0]] + [swap(grads[k], "peer", peers, k) for k in range(1, peers)]
    losses = [losses[0]] + [swap(losses[k], "peer", peers, k) for k in range(1, peers)]

    masks = jnp.array([0] + chips, jnp.int32)
    theirs = share((shard ^ 1) ^ masks, grads, head_weight, depth)
    given = swap(theirs, "vocab", shards, 1)
    mine = share(shard ^ masks, grads, head_weight, depth)
    coded = [
        swap(encode(mine, given, n + 1), "vocab", shards, mask) for n, mask in enumerate(chips)
    ]
    grad_hidden, token_loss = finish(own_arr, labels, mine, given, losses, coded)
    return grad_hidden, token_loss


def solution(mesh):
    in_specs = (P("peer", None, None), P("peer", None, "vocab"), P(), P())
    out_specs = (P("peer", None, "vocab"), P("peer", None))
    return jax.shard_map(on_device, mesh=mesh, in_specs=in_specs, out_specs=out_specs, check_vma=False)
```

```python
import functools
import jax
import jax.numpy as jnp
from jax import lax
from jax.experimental import pallas as pl
from jax.experimental.pallas import tpu as pltpu
from jax.sharding import PartitionSpec as P

SEGS = 8
IGNORED = 256
GROUP = 16
LANES = 128
PLAIN_CHUNKS = 4
IN_FLIGHT = 4
LOSS_TERMS = 3
CODE_ROWS = 16
CODE_STEPS = 64.0
CODE_TOP = 32766.0
LARGE = pltpu.CompilerParams(vmem_limit_bytes=32 * 1024 * 1024)
SMALL = pltpu.CompilerParams(vmem_limit_bytes=16 * 1024 * 1024)


def lane_ids(rows):
    return lax.broadcasted_iota(jnp.int32, (rows, LANES), 1)


def wanted_ranks(first, count, own, block):
    row = lax.broadcasted_iota(jnp.int32, (count, 1), 0) + first
    return (own ^ (row // block)) * block + row % block + 1


def ranks_along(labels):
    tokens = labels.shape[1]
    on = labels >= 0
    flags = jnp.broadcast_to(on.astype(jnp.float32), (8, tokens)).astype(jnp.bfloat16)
    src = lax.broadcasted_iota(jnp.int32, (tokens, tokens), 0)
    dst = lax.broadcasted_iota(jnp.int32, (tokens, tokens), 1)
    upto = (src <= dst).astype(jnp.float32).astype(jnp.bfloat16)
    rank = jnp.dot(flags, upto, preferred_element_type=jnp.float32)[0:1, :].astype(jnp.int32)
    return jnp.where(on, rank, 0)


def project_kernel(chunk_start, own_ref, shard_ref, lab_hbm, seg_hbm, hid_hbm, w_hbm, mine_ref, theirs_ref, meta_ref, *rest):
    out_refs, (lab_ref, seg_ref, hid_ref, few_ref, acc_ref, small_sem, hid_sem, w_sem) = rest[:-8], rest[-8:]
    tokens, depth = hid_ref.shape
    rows = few_ref.shape[0]
    block = out_refs[0].shape[0]
    part = depth // hid_sem.shape[0]
    spans = [pl.ds(n, part) for n in range(0, depth, part)]
    count, chunk, _ = mine_ref.shape
    targets = [(theirs_ref, 1, n) for n in range(count)] + [(mine_ref, 0, n) for n in range(count)]
    starts = [chunk_start(shard_ref[0], slot, n) for _, slot, n in targets]
    small = [
        pltpu.make_async_copy(lab_hbm, lab_ref, small_sem.at[0]),
        pltpu.make_async_copy(seg_hbm, seg_ref, small_sem.at[1]),
    ]
    hid_copies = [
        pltpu.make_async_copy(hid_hbm.at[0, :, span], hid_ref.at[:, span], hid_sem.at[n])
        for n, span in enumerate(spans)
    ]
    w_copies = [
        pltpu.make_async_copy(w_hbm.at[0, pl.ds(start, chunk), :], ref.at[n], w_sem.at[m])
        for m, (start, (ref, _, n)) in enumerate(zip(starts, targets))
    ]
    queue = small + hid_copies + w_copies
    for copy in queue[: 2 + IN_FLIGHT]:
        copy.start()
    queue = queue[2 + IN_FLIGHT :]
    for copy in small:
        copy.wait()

    lab = lab_ref[...]
    seg = seg_ref[...]
    rank = ranks_along(lab)
    pick = rank == wanted_ranks(0, rows, own_ref[0], block)
    picker = pick.astype(jnp.float32).astype(jnp.bfloat16)
    for copy, span in zip(hid_copies, spans):
        copy.wait()
        if queue:
            queue.pop(0).start()
        few = jnp.dot(picker, hid_ref[:, span], preferred_element_type=jnp.float32)
        few_ref[:, span] = few.astype(jnp.bfloat16)

    mine = pick[:block, :]
    label = jnp.sum(jnp.where(mine, lab, 0).astype(jnp.float32), axis=1, keepdims=True)
    doc = jnp.sum(jnp.where(mine, seg, 0).astype(jnp.float32), axis=1, keepdims=True)
    same = (lab >= 0) & (seg.astype(jnp.float32) == doc)
    count = jnp.sum(jnp.where(same, 1.0, 0.0), axis=1, keepdims=True)
    weight = float(tokens) / (SEGS * jnp.maximum(count, 1.0))
    lane = lane_ids(block)
    meta_ref[...] = jnp.where(lane == 0, label, jnp.where(lane == 1, weight, 0.0))

    for m, (copy, start, (ref, _, n)) in enumerate(zip(w_copies, starts, targets)):
        copy.wait()
        if queue:
            queue.pop(0).start()
        term = jnp.dot(few_ref[:, pl.ds(start, chunk)], ref[n], preferred_element_type=jnp.float32)
        if m == 0:
            acc_ref[...] = term
        elif m < len(targets) - 1:
            acc_ref[...] += term
        else:
            logits = (acc_ref[...] + term).astype(jnp.bfloat16)
            for k, out_ref in enumerate(out_refs):
                out_ref[...] = logits[k * block : (k + 1) * block, :]


def project(ids, labels, segments, hidden, head_weight, peers, chunk_start, count):
    tokens, depth = hidden.shape[1:]
    width = head_weight.shape[2]
    rows = tokens - IGNORED
    block = rows // peers
    hbm = pl.BlockSpec(memory_space=pltpu.HBM)
    vmem = pl.BlockSpec(memory_space=pltpu.VMEM)
    return pl.pallas_call(
        functools.partial(project_kernel, chunk_start),
        in_specs=[pl.BlockSpec(memory_space=pltpu.SMEM)] * 2 + [hbm] * 4,
        out_specs=[vmem] * (3 + peers),
        out_shape=[jax.ShapeDtypeStruct((count, depth // (2 * count), width), jnp.bfloat16)] * 2
        + [jax.ShapeDtypeStruct((block, LANES), jnp.float32)]
        + [jax.ShapeDtypeStruct((block, width), jnp.bfloat16)] * peers,
        scratch_shapes=[
            pltpu.VMEM((1, tokens), jnp.int32),
            pltpu.VMEM((1, tokens), jnp.int32),
            pltpu.VMEM((tokens, depth), jnp.bfloat16),
            pltpu.VMEM((rows, depth), jnp.bfloat16),
            pltpu.VMEM((rows, width), jnp.float32),
            pltpu.SemaphoreType.DMA((2,)),
            pltpu.SemaphoreType.DMA((4,)),
            pltpu.SemaphoreType.DMA((2 * count,)),
        ],
        compiler_params=LARGE,
        cost_estimate=pl.CostEstimate(
            flops=2 * rows * depth * (width + tokens), bytes_accessed=0, transcendentals=0
        ),
        name="project",
    )(*ids, labels, segments, hidden, head_weight)


def pair_list(peers):
    return [(i, j) for i in range(peers) for j in range(peers) if i != j]


def stat_slots(peers):
    pairs = pair_list(peers)
    return peers, {p: peers + n for n, p in enumerate(pairs)}, peers + len(pairs)


def stats_kernel(own_ref, shard_ref, meta_ref, *refs):
    logit_refs, out_ref = refs[:-1], refs[-1]
    peers = len(logit_refs)
    block, width = logit_refs[0].shape
    _, pair_slot, target_slot = stat_slots(peers)
    span = LANES * GROUP // block
    lane = lane_ids(GROUP)
    sums = jnp.zeros((GROUP, LANES), jnp.float32)
    peaks = jnp.zeros((GROUP, LANES), jnp.float32)
    for g in range(block // GROUP):
        rows = slice(g * GROUP, (g + 1) * GROUP)
        label = meta_ref[rows, 0:1].astype(jnp.int32) - shard_ref[0] * width
        peak = []
        for ref in logit_refs:
            top = ref[rows, 0:LANES].astype(jnp.float32)
            for c in range(LANES, width, LANES):
                top = jnp.maximum(top, ref[rows, c : c + LANES].astype(jnp.float32))
            peak.append(jnp.max(top, axis=1, keepdims=True))
        total = [jnp.zeros((GROUP, LANES), jnp.float32) for _ in range(peers)]
        target = [jnp.zeros((GROUP, LANES), jnp.float32) for _ in range(peers)]
        cross = {p: jnp.zeros((GROUP, LANES), jnp.float32) for p in pair_slot}
        for c in range(0, width, LANES):
            l = [ref[rows, c : c + LANES].astype(jnp.float32) for ref in logit_refs]
            e = [jnp.exp(l[k] - peak[k]) for k in range(peers)]
            hit = (lane + c) == label
            for i in range(peers):
                total[i] += e[i]
                target[i] += jnp.where(hit, l[i], 0.0)
                for j in range(i + 1, peers):
                    gap = l[i] - l[j]
                    cross[i, j] += e[i] * gap
                    cross[j, i] -= e[j] * gap

        def put(slot, vals, top):
            nonlocal sums, peaks
            here = lane == g * span + slot
            sums = jnp.where(here, jnp.sum(vals, axis=1, keepdims=True), sums)
            if top is not None:
                peaks = jnp.where(here, top, peaks)

        for i in range(peers):
            put(i, total[i], peak[i])
            put(target_slot + i, target[i], None)
        for (i, j), slot in pair_slot.items():
            put(slot, cross[i, j], peak[i])
    out_ref[0:GROUP, :] = sums
    out_ref[GROUP : 2 * GROUP, :] = peaks


def stats(ids, meta, logits):
    block, width = logits[0].shape
    peers = len(logits)
    return pl.pallas_call(
        stats_kernel,
        in_specs=[pl.BlockSpec(memory_space=pltpu.SMEM)] * 2 + [pl.BlockSpec(memory_space=pltpu.VMEM)] * (1 + peers),
        out_shape=jax.ShapeDtypeStruct((2 * GROUP, LANES), jnp.float32),
        compiler_params=SMALL,
        cost_estimate=pl.CostEstimate(
            flops=40 * block * width * peers, bytes_accessed=2 * block * width * peers, transcendentals=block * width * peers
        ),
        name="stats",
    )(*ids, meta, *logits)


def merged(parts):
    top = parts[0][GROUP:, :]
    for part in parts[1:]:
        top = jnp.maximum(top, part[GROUP:, :])
    total = jnp.zeros_like(top)
    for part in parts:
        total += part[:GROUP, :] * jnp.exp(part[GROUP:, :] - top)
    return total, top


def merge_kernel(*refs):
    total, top = merged([ref[...] for ref in refs[:-1]])
    refs[-1][:GROUP, :] = total
    refs[-1][GROUP:, :] = top


def merge(parts):
    return pl.pallas_call(
        merge_kernel,
        in_specs=[pl.BlockSpec(memory_space=pltpu.VMEM)] * len(parts),
        out_shape=jax.ShapeDtypeStruct(parts[0].shape, jnp.float32),
        compiler_params=SMALL,
        name="merge",
    )(*parts)


def grad_kernel(count, own_ref, shard_ref, meta_ref, *refs):
    stat_refs, refs = refs[:count], refs[count:]
    peers = len(refs) // 2
    logit_refs, grad_refs = refs[:peers], refs[peers:]
    block, width = logit_refs[0].shape
    _, pair_slot, target_slot = stat_slots(peers)
    span = LANES * GROUP // block
    lane = lane_ids(GROUP)
    total, top = merged([ref[...] for ref in stat_refs])
    norm = top + jnp.log(jnp.maximum(total, 1e-37))
    third = 1.0 / (peers - 1)
    for g in range(block // GROUP):
        rows = slice(g * GROUP, (g + 1) * GROUP)
        at = lambda array, slot: array[:, g * span + slot : g * span + slot + 1]
        label = meta_ref[rows, 0:1].astype(jnp.int32) - shard_ref[0] * width
        weight = meta_ref[rows, 1:2]
        inverse = [1.0 / at(total, i) for i in range(peers)]
        norms = [at(norm, i) for i in range(peers)]
        mean = {p: at(total, slot) * inverse[p[0]] for p, slot in pair_slot.items()}
        shift = []
        for i in range(peers):
            ahead = sum(mean[i, j] for j in range(peers) if j != i)
            back = sum(mean[j, i] for j in range(peers) if j != i)
            loss = norms[i] - at(total, target_slot + i) + (ahead + back) * third
            terms = jnp.zeros((GROUP, LANES), jnp.float32)
            for n in range(LOSS_TERMS):
                term = loss.astype(jnp.bfloat16).astype(jnp.float32)
                loss = loss - term
                terms = jnp.where(lane == n, term, terms)
            grad_refs[i][rows, width:] = terms.astype(jnp.bfloat16)
            shift.append(1.0 + (peers - ahead) * third)
        for c in range(0, width, LANES):
            l = [ref[rows, c : c + LANES].astype(jnp.float32) for ref in logit_refs]
            p = [jnp.exp(l[k] - norms[k]) for k in range(peers)]
            common = sum(l) * third
            rest = sum(p) * third + jnp.where((lane + c) == label, 1.0, 0.0)
            for i in range(peers):
                grad = p[i] * (shift[i] + (l[i] * (peers * third) - common)) - rest
                grad_refs[i][rows, c : c + LANES] = (weight * grad).astype(jnp.bfloat16)


def gradients(ids, meta, parts, logits):
    block, width = logits[0].shape
    peers = len(logits)
    return pl.pallas_call(
        functools.partial(grad_kernel, len(parts)),
        in_specs=[pl.BlockSpec(memory_space=pltpu.SMEM)] * 2
        + [pl.BlockSpec(memory_space=pltpu.VMEM)] * (1 + len(parts) + peers),
        out_shape=[jax.ShapeDtypeStruct((block, width + LANES), jnp.bfloat16)] * peers,
        compiler_params=SMALL,
        cost_estimate=pl.CostEstimate(
            flops=20 * block * width * peers, bytes_accessed=4 * block * width * peers, transcendentals=block * width * peers
        ),
        name="gradients",
    )(*ids, meta, *parts, *logits)


def share_of(w_ref, index, grad):
    return lax.dot_general(w_ref[index], grad, (((1,), (1,)), ((), ())), preferred_element_type=jnp.float32)


def both_shares(mask, shard_ref, refs):
    mine_ref, theirs_ref, own_ref, other_ref = refs
    index = (shard_ref[0] // 2) ^ mask
    return share_of(mine_ref, index, own_ref[...]) + share_of(theirs_ref, index, other_ref[...])


def gather_kernel(peers, own_ref, shard_ref, *refs):
    block_refs, (own_all, other_all, loss_ref) = refs[:-3], refs[-3:]
    block, width = block_refs[0].shape[0], own_all.shape[1]
    for k in range(peers):
        rows = slice(k * block, (k + 1) * block)
        own_all[rows, :] = block_refs[k][:, :width]
        other_all[rows, :] = block_refs[peers + k][:, :width]
        loss_ref[rows, :] = jnp.sum(block_refs[k][:, width:].astype(jnp.float32), axis=1, keepdims=True)


def vmem_call(kernel, outs, cost, name, ids, *arrays):
    return pl.pallas_call(
        kernel,
        in_specs=[pl.BlockSpec(memory_space=pltpu.SMEM)] * 2 + [pl.BlockSpec(memory_space=pltpu.VMEM)] * len(arrays),
        out_specs=[pl.BlockSpec(memory_space=pltpu.VMEM)] * len(outs),
        out_shape=[jax.ShapeDtypeStruct(shape, dtype) for shape, dtype in outs],
        compiler_params=SMALL,
        cost_estimate=cost,
        name=name,
    )(*ids, *arrays)


def coded(value):
    depth, rows = value.shape
    top = jnp.maximum(jnp.max(jnp.abs(value), axis=0, keepdims=True), 1e-30)
    code = jnp.ceil(jnp.log2(top) * CODE_STEPS)
    unit = jnp.exp2(code * (-1.0 / CODE_STEPS)) * CODE_TOP
    whole = jnp.clip(jnp.round(value * unit), -CODE_TOP - 1, CODE_TOP + 1)
    codes = jnp.broadcast_to(code, (CODE_ROWS, rows))
    return whole.astype(jnp.int32).astype(jnp.int16), codes.astype(jnp.int32).astype(jnp.int16)


def put_coded(ref, value):
    depth = value.shape[0]
    ref[:depth, :], ref[depth:, :] = coded(value)


def get_coded(ref):
    depth = ref.shape[0] - CODE_ROWS
    code = ref[depth:, :].astype(jnp.int32).astype(jnp.float32)[0:1, :]
    unit = jnp.exp2(code * (1.0 / CODE_STEPS)) * (1.0 / CODE_TOP)
    return ref[:depth, :].astype(jnp.int32).astype(jnp.float32) * unit


def encode_kernel(mask, own_ref, shard_ref, *refs):
    value = both_shares(mask, shard_ref, refs[:4])
    put_coded(refs[4], value)
    for ref in refs[5:]:
        ref[...] = value


def relay_kernel(own_ref, shard_ref, value_ref, coded_ref, out_ref):
    put_coded(out_ref, value_ref[...] + get_coded(coded_ref))


def keep_kernel(own_ref, shard_ref, *refs):
    refs[-1][...] = both_shares(0, shard_ref, refs[:-1])


def place_kernel(peers, own_ref, shard_ref, row_ref, loss_ref, place_ref, out_ref):
    tokens, rows = place_ref.shape
    block = rows // peers
    rank = ranks_along(row_ref[...])
    here = rank == wanted_ranks(0, rows, own_ref[0], block)
    out_ref[...] = jnp.sum(jnp.where(here, loss_ref[...], 0.0), axis=0, keepdims=True)

    src = lax.broadcasted_iota(jnp.int32, (tokens, tokens), 0)
    dst = lax.broadcasted_iota(jnp.int32, (tokens, tokens), 1)
    flags = (row_ref[...] >= 0).astype(jnp.float32).astype(jnp.bfloat16)
    flags = jnp.broadcast_to(flags, (LANES, tokens))
    turned = lambda keep: lax.dot_general(
        keep.astype(jnp.float32).astype(jnp.bfloat16),
        flags,
        (((1,), (1,)), ((), ())),
        preferred_element_type=jnp.float32,
    )[:, 0:1]
    rank = (turned(dst <= src) * turned(dst == src)).astype(jnp.int32)
    col = lax.broadcasted_iota(jnp.int32, (1, rows), 1)
    wanted = (own_ref[0] ^ (col // block)) * block + col % block + 1
    place_ref[...] = (rank == wanted).astype(jnp.float32).astype(jnp.bfloat16)


def place(ids, labels, losses, peers):
    tokens = labels.shape[1]
    return vmem_call(
        functools.partial(place_kernel, peers),
        [((tokens, tokens - IGNORED), jnp.bfloat16), ((1, tokens), jnp.float32)],
        pl.CostEstimate(flops=4 * tokens * tokens * LANES, bytes_accessed=0, transcendentals=0),
        "place",
        ids,
        labels,
        losses,
    )


def finish_kernel(own_ref, shard_ref, place_ref, sum_ref, *refs):
    value = sum_ref[...]
    for ref in refs[:-1]:
        value += get_coded(ref)
    result = None
    for _ in range(3):
        piece = value.astype(jnp.bfloat16)
        value = value - piece.astype(jnp.float32)
        term = lax.dot_general(
            place_ref[...], piece, (((1,), (1,)), ((), ())), preferred_element_type=jnp.float32
        )
        result = term if result is None else result + term
    refs[-1][0] = result


def swap(array, axis, size, mask):
    return lax.ppermute(array, axis, [(i, i ^ mask) for i in range(size)])


def hop(array, pairs):
    return lax.ppermute(array, "vocab", [(2 * a + c, 2 * b + c) for a, b in pairs for c in range(2)])


def on_device(hidden, head_weight, labels, segments):
    peers = lax.axis_size("peer")
    shards = lax.axis_size("vocab")
    width = head_weight.shape[2]
    depth = head_weight.shape[1] // shards
    tokens = labels.shape[0]
    rows = tokens - IGNORED
    chips = shards // 2
    labels, segments = labels[None, :], segments[None, :]
    ids = [lax.axis_index(name).astype(jnp.int32).reshape(1) for name in ("peer", "vocab")]
    by_core = depth % LANES == 0

    def chunk_start(shard, slot, n):
        if by_core:
            return pl.multiple_of((2 * n + ((shard % 2) ^ slot)) * depth, depth)
        return (n + slot * PLAIN_CHUNKS) * (head_weight.shape[1] // (2 * PLAIN_CHUNKS))

    in_hbm = [pltpu.with_memory_space_constraint(x, pltpu.HBM) for x in (labels, segments, hidden, head_weight)]
    w_mine, w_theirs, meta, *blocks = project(
        ids, *in_hbm, peers, chunk_start, chips if by_core else PLAIN_CHUNKS
    )

    def across(arrays):
        moved = {k: swap(arrays[k], "peer", peers, k) for k in range(peers - 1, 0, -1)}
        return [arrays[0]] + [moved[k] for k in range(1, peers)]

    core_swap = lambda array: swap(array, "vocab", shards, 1)
    logits = across(blocks)
    part = stats(ids, meta, logits)
    part = merge([part, core_swap(part)])
    parts = [part] + [swap(part, "vocab", shards, 2 * mask) for mask in range(1, chips)]
    grads = across(gradients(ids, meta, parts, logits))

    cost = pl.CostEstimate(flops=1000, bytes_accessed=0, transcendentals=0)
    flat = ((rows, width), jnp.bfloat16)
    kernel = functools.partial(gather_kernel, peers)
    outs = [flat, flat, ((rows, 1), jnp.float32)]
    others = [core_swap(grad) for grad in grads]
    own_grad, other_grad, losses = vmem_call(kernel, outs, cost, "gather", ids, *grads, *others)
    placing, token_loss = place(ids, labels, losses, peers)
    if by_core:
        operands = (w_mine, core_swap(w_theirs), own_grad, other_grad)
        coded_shape, full = ((depth + CODE_ROWS, rows), jnp.int16), ((depth, rows), jnp.float32)

        def encode(mask, *more):
            kernel = functools.partial(encode_kernel, mask)
            return vmem_call(kernel, [coded_shape, *more], cost, "encode", ids, *operands)

        if chips == 4:
            (three,) = encode(3)
            far, mid = hop(three, [(0, 1), (3, 2)]), hop(three, [(1, 2), (2, 1)])
            two, two_sum = encode(2, full)
            skip = hop(two, [(0, 2), (3, 1)])
            (one,) = encode(1)
            (relayed,) = vmem_call(relay_kernel, [coded_shape], cost, "relay", ids, two_sum, far)
            relay = hop(relayed, [(1, 3), (2, 0)])
            one = lax.optimization_barrier((one, relayed))[0]
            near = hop(one, [(0, 1), (1, 0), (2, 3), (3, 2)])
            arrived = [mid, skip, relay, near]
        else:
            arrived = [swap(encode(mask)[0], "vocab", shards, 2 * mask) for mask in range(chips - 1, 0, -1)]
        (kept,) = vmem_call(keep_kernel, [((depth, rows), jnp.float32)], cost, "keep", ids, *operands)
    else:
        arrived = []
        share = lax.dot_general(
            head_weight[0], own_grad, (((1,), (1,)), ((), ())), preferred_element_type=jnp.float32
        )
        kept = lax.psum_scatter(share, "vocab", scatter_dimension=0, tiled=True)
    out = ((1, tokens, depth), jnp.float32)
    (grad_hidden,) = vmem_call(finish_kernel, [out], cost, "finish", ids, placing, kept, *arrived)
    return grad_hidden, token_loss


def solution(mesh):
    in_specs = (P("peer", None, None), P("peer", None, "vocab"), P(), P())
    out_specs = (P("peer", None, "vocab"), P("peer", None))
    return jax.shard_map(on_device, mesh=mesh, in_specs=in_specs, out_specs=out_specs, check_vma=False)
```

```python
import functools
import jax
import jax.numpy as jnp
from jax import lax
from jax.experimental import pallas as pl
from jax.experimental.pallas import tpu as pltpu
from jax.sharding import PartitionSpec as P

SEGS = 8
IGNORED = 256
GROUP = 16
LANES = 128
PLAIN_CHUNKS = 4
IN_FLIGHT = 4
LOSS_TERMS = 3
CODE_ROWS = 16
CODE_STEPS = 64.0
CODE_TOP = 32766.0
LARGE = pltpu.CompilerParams(vmem_limit_bytes=32 * 1024 * 1024)
SMALL = pltpu.CompilerParams(vmem_limit_bytes=16 * 1024 * 1024)


def lane_ids(rows):
    return lax.broadcasted_iota(jnp.int32, (rows, LANES), 1)


def wanted_ranks(first, count, own, block):
    row = lax.broadcasted_iota(jnp.int32, (count, 1), 0) + first
    return (own ^ (row // block)) * block + row % block + 1


def ranks_along(labels):
    tokens = labels.shape[1]
    on = labels >= 0
    flags = jnp.broadcast_to(on.astype(jnp.float32), (8, tokens)).astype(jnp.bfloat16)
    src = lax.broadcasted_iota(jnp.int32, (tokens, tokens), 0)
    dst = lax.broadcasted_iota(jnp.int32, (tokens, tokens), 1)
    upto = (src <= dst).astype(jnp.float32).astype(jnp.bfloat16)
    rank = jnp.dot(flags, upto, preferred_element_type=jnp.float32)[0:1, :].astype(jnp.int32)
    return jnp.where(on, rank, 0)


def project_kernel(chunk_start, own_ref, shard_ref, lab_hbm, seg_hbm, hid_hbm, w_hbm, mine_ref, theirs_ref, meta_ref, *rest):
    out_refs, (lab_ref, seg_ref, hid_ref, few_ref, acc_ref, small_sem, hid_sem, w_sem) = rest[:-8], rest[-8:]
    tokens, depth = hid_ref.shape
    rows = few_ref.shape[0]
    block = out_refs[0].shape[0]
    part = depth // hid_sem.shape[0]
    spans = [pl.ds(n, part) for n in range(0, depth, part)]
    count, chunk, _ = mine_ref.shape
    targets = [(theirs_ref, 1, n) for n in range(count)] + [(mine_ref, 0, n) for n in range(count)]
    starts = [chunk_start(shard_ref[0], slot, n) for _, slot, n in targets]
    small = [
        pltpu.make_async_copy(lab_hbm, lab_ref, small_sem.at[0]),
        pltpu.make_async_copy(seg_hbm, seg_ref, small_sem.at[1]),
    ]
    hid_copies = [
        pltpu.make_async_copy(hid_hbm.at[0, :, span], hid_ref.at[:, span], hid_sem.at[n])
        for n, span in enumerate(spans)
    ]
    w_copies = [
        pltpu.make_async_copy(w_hbm.at[0, pl.ds(start, chunk), :], ref.at[n], w_sem.at[m])
        for m, (start, (ref, _, n)) in enumerate(zip(starts, targets))
    ]
    queue = small + hid_copies + w_copies
    for copy in queue[: 2 + IN_FLIGHT]:
        copy.start()
    queue = queue[2 + IN_FLIGHT :]
    for copy in small:
        copy.wait()

    lab = lab_ref[...]
    seg = seg_ref[...]
    rank = ranks_along(lab)
    pick = rank == wanted_ranks(0, rows, own_ref[0], block)
    picker = pick.astype(jnp.float32).astype(jnp.bfloat16)
    for copy, span in zip(hid_copies, spans):
        copy.wait()
        if queue:
            queue.pop(0).start()
        few = jnp.dot(picker, hid_ref[:, span], preferred_element_type=jnp.float32)
        few_ref[:, span] = few.astype(jnp.bfloat16)

    mine = pick[:block, :]
    label = jnp.sum(jnp.where(mine, lab, 0).astype(jnp.float32), axis=1, keepdims=True)
    doc = jnp.sum(jnp.where(mine, seg, 0).astype(jnp.float32), axis=1, keepdims=True)
    same = (lab >= 0) & (seg.astype(jnp.float32) == doc)
    count = jnp.sum(jnp.where(same, 1.0, 0.0), axis=1, keepdims=True)
    weight = float(tokens) / (SEGS * jnp.maximum(count, 1.0))
    lane = lane_ids(block)
    meta_ref[...] = jnp.where(lane == 0, label, jnp.where(lane == 1, weight, 0.0))

    for m, (copy, start, (ref, _, n)) in enumerate(zip(w_copies, starts, targets)):
        copy.wait()
        if queue:
            queue.pop(0).start()
        term = jnp.dot(few_ref[:, pl.ds(start, chunk)], ref[n], preferred_element_type=jnp.float32)
        if m == 0:
            acc_ref[...] = term
        elif m < len(targets) - 1:
            acc_ref[...] += term
        else:
            logits = (acc_ref[...] + term).astype(jnp.bfloat16)
            for k, out_ref in enumerate(out_refs):
                out_ref[...] = logits[k * block : (k + 1) * block, :]


def project(ids, labels, segments, hidden, head_weight, peers, chunk_start, count):
    tokens, depth = hidden.shape[1:]
    width = head_weight.shape[2]
    rows = tokens - IGNORED
    block = rows // peers
    hbm = pl.BlockSpec(memory_space=pltpu.HBM)
    vmem = pl.BlockSpec(memory_space=pltpu.VMEM)
    return pl.pallas_call(
        functools.partial(project_kernel, chunk_start),
        in_specs=[pl.BlockSpec(memory_space=pltpu.SMEM)] * 2 + [hbm] * 4,
        out_specs=[vmem] * (3 + peers),
        out_shape=[jax.ShapeDtypeStruct((count, depth // (2 * count), width), jnp.bfloat16)] * 2
        + [jax.ShapeDtypeStruct((block, LANES), jnp.float32)]
        + [jax.ShapeDtypeStruct((block, width), jnp.bfloat16)] * peers,
        scratch_shapes=[
            pltpu.VMEM((1, tokens), jnp.int32),
            pltpu.VMEM((1, tokens), jnp.int32),
            pltpu.VMEM((tokens, depth), jnp.bfloat16),
            pltpu.VMEM((rows, depth), jnp.bfloat16),
            pltpu.VMEM((rows, width), jnp.float32),
            pltpu.SemaphoreType.DMA((2,)),
            pltpu.SemaphoreType.DMA((2,)),
            pltpu.SemaphoreType.DMA((2 * count,)),
        ],
        compiler_params=LARGE,
        cost_estimate=pl.CostEstimate(
            flops=2 * rows * depth * (width + tokens), bytes_accessed=0, transcendentals=0
        ),
        name="project",
    )(*ids, labels, segments, hidden, head_weight)


def pair_list(peers):
    return [(i, j) for i in range(peers) for j in range(peers) if i != j]


def stat_slots(peers):
    pairs = pair_list(peers)
    return peers, {p: peers + n for n, p in enumerate(pairs)}, peers + len(pairs)


def stats_kernel(own_ref, shard_ref, meta_ref, *refs):
    logit_refs, out_ref = refs[:-1], refs[-1]
    peers = len(logit_refs)
    block, width = logit_refs[0].shape
    _, pair_slot, target_slot = stat_slots(peers)
    span = LANES * GROUP // block
    lane = lane_ids(GROUP)
    sums = jnp.zeros((GROUP, LANES), jnp.float32)
    peaks = jnp.zeros((GROUP, LANES), jnp.float32)
    for g in range(block // GROUP):
        rows = slice(g * GROUP, (g + 1) * GROUP)
        label = meta_ref[rows, 0:1].astype(jnp.int32) - shard_ref[0] * width
        peak = []
        for ref in logit_refs:
            top = ref[rows, 0:LANES].astype(jnp.float32)
            for c in range(LANES, width, LANES):
                top = jnp.maximum(top, ref[rows, c : c + LANES].astype(jnp.float32))
            peak.append(jnp.max(top, axis=1, keepdims=True))
        total = [jnp.zeros((GROUP, LANES), jnp.float32) for _ in range(peers)]
        target = [jnp.zeros((GROUP, LANES), jnp.float32) for _ in range(peers)]
        cross = {p: jnp.zeros((GROUP, LANES), jnp.float32) for p in pair_slot}
        for c in range(0, width, LANES):
            l = [ref[rows, c : c + LANES].astype(jnp.float32) for ref in logit_refs]
            e = [jnp.exp(l[k] - peak[k]) for k in range(peers)]
            hit = (lane + c) == label
            for i in range(peers):
                total[i] += e[i]
                target[i] += jnp.where(hit, l[i], 0.0)
                for j in range(i + 1, peers):
                    gap = l[i] - l[j]
                    cross[i, j] += e[i] * gap
                    cross[j, i] -= e[j] * gap

        def put(slot, vals, top):
            nonlocal sums, peaks
            here = lane == g * span + slot
            sums = jnp.where(here, jnp.sum(vals, axis=1, keepdims=True), sums)
            if top is not None:
                peaks = jnp.where(here, top, peaks)

        for i in range(peers):
            put(i, total[i], peak[i])
            put(target_slot + i, target[i], None)
        for (i, j), slot in pair_slot.items():
            put(slot, cross[i, j], peak[i])
    out_ref[0:GROUP, :] = sums
    out_ref[GROUP : 2 * GROUP, :] = peaks


def stats(ids, meta, logits):
    block, width = logits[0].shape
    peers = len(logits)
    return pl.pallas_call(
        stats_kernel,
        in_specs=[pl.BlockSpec(memory_space=pltpu.SMEM)] * 2 + [pl.BlockSpec(memory_space=pltpu.VMEM)] * (1 + peers),
        out_shape=jax.ShapeDtypeStruct((2 * GROUP, LANES), jnp.float32),
        compiler_params=SMALL,
        cost_estimate=pl.CostEstimate(
            flops=40 * block * width * peers, bytes_accessed=2 * block * width * peers, transcendentals=block * width * peers
        ),
        name="stats",
    )(*ids, meta, *logits)


def merged(parts):
    top = parts[0][GROUP:, :]
    for part in parts[1:]:
        top = jnp.maximum(top, part[GROUP:, :])
    total = jnp.zeros_like(top)
    for part in parts:
        total += part[:GROUP, :] * jnp.exp(part[GROUP:, :] - top)
    return total, top


def merge_kernel(*refs):
    total, top = merged([ref[...] for ref in refs[:-1]])
    refs[-1][:GROUP, :] = total
    refs[-1][GROUP:, :] = top


def merge(parts):
    return pl.pallas_call(
        merge_kernel,
        in_specs=[pl.BlockSpec(memory_space=pltpu.VMEM)] * len(parts),
        out_shape=jax.ShapeDtypeStruct(parts[0].shape, jnp.float32),
        compiler_params=SMALL,
        name="merge",
    )(*parts)


def grad_kernel(count, own_ref, shard_ref, meta_ref, *refs):
    stat_refs, refs = refs[:count], refs[count:]
    peers = len(refs) // 2
    logit_refs, grad_refs = refs[:peers], refs[peers:]
    block, width = logit_refs[0].shape
    _, pair_slot, target_slot = stat_slots(peers)
    span = LANES * GROUP // block
    lane = lane_ids(GROUP)
    total, top = merged([ref[...] for ref in stat_refs])
    norm = top + jnp.log(jnp.maximum(total, 1e-37))
    third = 1.0 / (peers - 1)
    for g in range(block // GROUP):
        rows = slice(g * GROUP, (g + 1) * GROUP)
        at = lambda array, slot: array[:, g * span + slot : g * span + slot + 1]
        label = meta_ref[rows, 0:1].astype(jnp.int32) - shard_ref[0] * width
        weight = meta_ref[rows, 1:2]
        inverse = [1.0 / at(total, i) for i in range(peers)]
        norms = [at(norm, i) for i in range(peers)]
        mean = {p: at(total, slot) * inverse[p[0]] for p, slot in pair_slot.items()}
        shift = []
        for i in range(peers):
            ahead = sum(mean[i, j] for j in range(peers) if j != i)
            back = sum(mean[j, i] for j in range(peers) if j != i)
            loss = norms[i] - at(total, target_slot + i) + (ahead + back) * third
            terms = jnp.zeros((GROUP, LANES), jnp.float32)
            for n in range(LOSS_TERMS):
                term = loss.astype(jnp.bfloat16).astype(jnp.float32)
                loss = loss - term
                terms = jnp.where(lane == n, term, terms)
            grad_refs[i][rows, width:] = terms.astype(jnp.bfloat16)
            shift.append(1.0 + (peers - ahead) * third)
        for c in range(0, width, LANES):
            l = [ref[rows, c : c + LANES].astype(jnp.float32) for ref in logit_refs]
            p = [jnp.exp(l[k] - norms[k]) for k in range(peers)]
            common = sum(l) * third
            rest = sum(p) * third + jnp.where((lane + c) == label, 1.0, 0.0)
            for i in range(peers):
                grad = p[i] * (shift[i] + (l[i] * (peers * third) - common)) - rest
                grad_refs[i][rows, c : c + LANES] = (weight * grad).astype(jnp.bfloat16)


def gradients(ids, meta, parts, logits):
    block, width = logits[0].shape
    peers = len(logits)
    return pl.pallas_call(
        functools.partial(grad_kernel, len(parts)),
        in_specs=[pl.BlockSpec(memory_space=pltpu.SMEM)] * 2
        + [pl.BlockSpec(memory_space=pltpu.VMEM)] * (1 + len(parts) + peers),
        out_shape=[jax.ShapeDtypeStruct((block, width + LANES), jnp.bfloat16)] * peers,
        compiler_params=SMALL,
        cost_estimate=pl.CostEstimate(
            flops=20 * block * width * peers, bytes_accessed=4 * block * width * peers, transcendentals=block * width * peers
        ),
        name="gradients",
    )(*ids, meta, *parts, *logits)


def share_of(w_ref, index, grad):
    return lax.dot_general(w_ref[index], grad, (((1,), (1,)), ((), ())), preferred_element_type=jnp.float32)


def both_shares(mask, shard_ref, refs):
    mine_ref, theirs_ref, own_ref, other_ref = refs
    index = (shard_ref[0] // 2) ^ mask
    return share_of(mine_ref, index, own_ref[...]) + share_of(theirs_ref, index, other_ref[...])


def gather_kernel(peers, own_ref, shard_ref, *refs):
    block_refs, (own_all, other_all, loss_ref) = refs[:-3], refs[-3:]
    block, width = block_refs[0].shape[0], own_all.shape[1]
    for k in range(peers):
        rows = slice(k * block, (k + 1) * block)
        own_all[rows, :] = block_refs[k][:, :width]
        other_all[rows, :] = block_refs[peers + k][:, :width]
        loss_ref[rows, :] = jnp.sum(block_refs[k][:, width:].astype(jnp.float32), axis=1, keepdims=True)


def vmem_call(kernel, outs, cost, name, ids, *arrays):
    return pl.pallas_call(
        kernel,
        in_specs=[pl.BlockSpec(memory_space=pltpu.SMEM)] * 2 + [pl.BlockSpec(memory_space=pltpu.VMEM)] * len(arrays),
        out_specs=[pl.BlockSpec(memory_space=pltpu.VMEM)] * len(outs),
        out_shape=[jax.ShapeDtypeStruct(shape, dtype) for shape, dtype in outs],
        compiler_params=SMALL,
        cost_estimate=cost,
        name=name,
    )(*ids, *arrays)


def coded(value):
    depth, rows = value.shape
    top = jnp.maximum(jnp.max(jnp.abs(value), axis=0, keepdims=True), 1e-30)
    code = jnp.ceil(jnp.log2(top) * CODE_STEPS)
    unit = jnp.exp2(code * (-1.0 / CODE_STEPS)) * CODE_TOP
    whole = jnp.clip(jnp.round(value * unit), -CODE_TOP - 1, CODE_TOP + 1)
    codes = jnp.broadcast_to(code, (CODE_ROWS, rows))
    return whole.astype(jnp.int32).astype(jnp.int16), codes.astype(jnp.int32).astype(jnp.int16)


def put_coded(ref, value):
    depth = value.shape[0]
    ref[:depth, :], ref[depth:, :] = coded(value)


def get_coded(ref):
    depth = ref.shape[0] - CODE_ROWS
    code = ref[depth:, :].astype(jnp.int32).astype(jnp.float32)[0:1, :]
    unit = jnp.exp2(code * (1.0 / CODE_STEPS)) * (1.0 / CODE_TOP)
    return ref[:depth, :].astype(jnp.int32).astype(jnp.float32) * unit


def encode_kernel(mask, own_ref, shard_ref, *refs):
    value = both_shares(mask, shard_ref, refs[:4])
    put_coded(refs[4], value)
    for ref in refs[5:]:
        ref[...] = value


def relay_kernel(own_ref, shard_ref, value_ref, coded_ref, out_ref):
    put_coded(out_ref, value_ref[...] + get_coded(coded_ref))


def keep_kernel(own_ref, shard_ref, *refs):
    value = both_shares(0, shard_ref, refs[:4])
    for ref in refs[4:-1]:
        value += get_coded(ref)
    refs[-1][...] = value


def place_kernel(peers, own_ref, shard_ref, row_ref, loss_ref, place_ref, out_ref):
    tokens, rows = place_ref.shape
    block = rows // peers
    rank = ranks_along(row_ref[...])
    here = rank == wanted_ranks(0, rows, own_ref[0], block)
    out_ref[...] = jnp.sum(jnp.where(here, loss_ref[...], 0.0), axis=0, keepdims=True)

    src = lax.broadcasted_iota(jnp.int32, (tokens, tokens), 0)
    dst = lax.broadcasted_iota(jnp.int32, (tokens, tokens), 1)
    flags = (row_ref[...] >= 0).astype(jnp.float32).astype(jnp.bfloat16)
    flags = jnp.broadcast_to(flags, (LANES, tokens))
    turned = lambda keep: lax.dot_general(
        keep.astype(jnp.float32).astype(jnp.bfloat16),
        flags,
        (((1,), (1,)), ((), ())),
        preferred_element_type=jnp.float32,
    )[:, 0:1]
    rank = (turned(dst <= src) * turned(dst == src)).astype(jnp.int32)
    col = lax.broadcasted_iota(jnp.int32, (1, rows), 1)
    wanted = (own_ref[0] ^ (col // block)) * block + col % block + 1
    place_ref[...] = (rank == wanted).astype(jnp.float32).astype(jnp.bfloat16)


def place(ids, labels, losses, peers):
    tokens = labels.shape[1]
    return vmem_call(
        functools.partial(place_kernel, peers),
        [((tokens, tokens - IGNORED), jnp.bfloat16), ((1, tokens), jnp.float32)],
        pl.CostEstimate(flops=4 * tokens * tokens * LANES, bytes_accessed=0, transcendentals=0),
        "place",
        ids,
        labels,
        losses,
    )


def finish_kernel(place_ref, sum_ref, *refs):
    coded_refs, (out_hbm, out_ref, sems) = refs[:-3], refs[-3:]
    value = sum_ref[...]
    for ref in coded_refs:
        value += get_coded(ref)
    high = value.astype(jnp.bfloat16)
    low = (value - high.astype(jnp.float32)).astype(jnp.bfloat16)
    turned = lambda place, piece: lax.dot_general(
        place, piece, (((1,), (1,)), ((), ())), preferred_element_type=jnp.float32
    )
    part = out_ref.shape[0] // sems.shape[0]
    copies = []
    for n in range(sems.shape[0]):
        span = pl.ds(n * part, part)
        place = place_ref[span, :]
        out_ref[span, :] = turned(place, high) + turned(place, low)
        copies.append(pltpu.make_async_copy(out_ref.at[span, :], out_hbm.at[0, span, :], sems.at[n]))
        copies[-1].start()
    for copy in copies:
        copy.wait()


def finish(placing, kept, arrived):
    tokens, rows = placing.shape
    depth = kept.shape[0]
    return pl.pallas_call(
        finish_kernel,
        in_specs=[pl.BlockSpec(memory_space=pltpu.VMEM)] * (2 + len(arrived)),
        out_specs=pl.BlockSpec(memory_space=pltpu.HBM),
        out_shape=jax.ShapeDtypeStruct((1, tokens, depth), jnp.float32),
        scratch_shapes=[pltpu.VMEM((tokens, depth), jnp.float32), pltpu.SemaphoreType.DMA((4,))],
        compiler_params=SMALL,
        cost_estimate=pl.CostEstimate(flops=1000, bytes_accessed=0, transcendentals=0),
        name="finish",
    )(placing, kept, *arrived)


def swap(array, axis, size, mask):
    return lax.ppermute(array, axis, [(i, i ^ mask) for i in range(size)])


def hop(array, pairs):
    return lax.ppermute(array, "vocab", [(2 * a + c, 2 * b + c) for a, b in pairs for c in range(2)])


def on_device(hidden, head_weight, labels, segments):
    peers = lax.axis_size("peer")
    shards = lax.axis_size("vocab")
    width = head_weight.shape[2]
    depth = head_weight.shape[1] // shards
    tokens = labels.shape[0]
    rows = tokens - IGNORED
    chips = shards // 2
    labels, segments = labels[None, :], segments[None, :]
    ids = [lax.axis_index(name).astype(jnp.int32).reshape(1) for name in ("peer", "vocab")]
    by_core = depth % LANES == 0

    def chunk_start(shard, slot, n):
        if by_core:
            return pl.multiple_of((2 * n + ((shard % 2) ^ slot)) * depth, depth)
        return (n + slot * PLAIN_CHUNKS) * (head_weight.shape[1] // (2 * PLAIN_CHUNKS))

    in_hbm = [pltpu.with_memory_space_constraint(x, pltpu.HBM) for x in (labels, segments, hidden, head_weight)]
    w_mine, w_theirs, meta, *blocks = project(
        ids, *in_hbm, peers, chunk_start, chips if by_core else PLAIN_CHUNKS
    )

    def across(arrays):
        moved = {k: swap(arrays[k], "peer", peers, k) for k in range(peers - 1, 0, -1)}
        return [arrays[0]] + [moved[k] for k in range(1, peers)]

    core_swap = lambda array: swap(array, "vocab", shards, 1)
    logits = across(blocks)
    part = stats(ids, meta, logits)
    part = merge([part, core_swap(part)])
    after = lambda array, *before: lax.optimization_barrier((array,) + before)[0]
    w_given = core_swap(after(w_theirs, part)) if by_core else None
    parts = [part] + [swap(part, "vocab", shards, 2 * mask) for mask in range(chips - 1, 0, -1)]
    grads = across(gradients(ids, meta, parts, logits))

    cost = pl.CostEstimate(flops=1000, bytes_accessed=0, transcendentals=0)
    flat = ((rows, width), jnp.bfloat16)
    kernel = functools.partial(gather_kernel, peers)
    outs = [flat, flat, ((rows, 1), jnp.float32)]
    others = [core_swap(grad) for grad in grads]
    own_grad, other_grad, losses = vmem_call(kernel, outs, cost, "gather", ids, *grads, *others)
    placing, token_loss = place(ids, labels, losses, peers)
    if by_core:
        operands = (w_mine, w_given, own_grad, other_grad)
        coded_shape, full = ((depth + CODE_ROWS, rows), jnp.int16), ((depth, rows), jnp.float32)

        def encode(mask, *more):
            kernel = functools.partial(encode_kernel, mask)
            return vmem_call(kernel, [coded_shape, *more], cost, "encode", ids, *operands)

        if chips == 4:
            (three,) = encode(3)
            far, mid = hop(three, [(0, 1), (3, 2)]), hop(three, [(1, 2), (2, 1)])
            two, two_sum = encode(2, full)
            skip = hop(two, [(0, 2), (3, 1)])
            (one,) = encode(1)
            (relayed,) = vmem_call(relay_kernel, [coded_shape], cost, "relay", ids, two_sum, far)
            relay = hop(relayed, [(1, 3), (2, 0)])
            one = lax.optimization_barrier((one, relayed))[0]
            near = hop(one, [(0, 1), (1, 0), (2, 3), (3, 2)])
            early, arrived = [mid, skip], [relay, near]
        else:
            early = []
            arrived = [swap(encode(mask)[0], "vocab", shards, 2 * mask) for mask in range(chips - 1, 0, -1)]
        (kept,) = vmem_call(keep_kernel, [((depth, rows), jnp.float32)], cost, "keep", ids, *operands, *early)
    else:
        arrived = []
        share = lax.dot_general(
            head_weight[0], own_grad, (((1,), (1,)), ((), ())), preferred_element_type=jnp.float32
        )
        kept = lax.psum_scatter(share, "vocab", scatter_dimension=0, tiled=True)
    grad_hidden = finish(placing, kept, arrived)
    return grad_hidden, token_loss


def solution(mesh):
    in_specs = (P("peer", None, None), P("peer", None, "vocab"), P(), P())
    out_specs = (P("peer", None, "vocab"), P("peer", None))
    return jax.shard_map(on_device, mesh=mesh, in_specs=in_specs, out_specs=out_specs, check_vma=False)
```

```python
import functools
import jax
import jax.numpy as jnp
from jax import lax
from jax.experimental import pallas as pl
from jax.experimental.pallas import tpu as pltpu
from jax.sharding import PartitionSpec as P

SEGS = 8
IGNORED = 256
GROUP = 16
LANES = 128
PLAIN_CHUNKS = 4
IN_FLIGHT = 4
LOSS_TERMS = 3
CODE_ROWS = 16
CODE_STEPS = 64.0
CODE_TOP = 32766.0
LARGE = pltpu.CompilerParams(vmem_limit_bytes=32 * 1024 * 1024)
SMALL = pltpu.CompilerParams(vmem_limit_bytes=16 * 1024 * 1024)


def lane_ids(rows):
    return lax.broadcasted_iota(jnp.int32, (rows, LANES), 1)


def wanted_ranks(first, count, own, block):
    row = lax.broadcasted_iota(jnp.int32, (count, 1), 0) + first
    return (own ^ (row // block)) * block + row % block + 1


def ranks_along(labels):
    tokens = labels.shape[1]
    on = labels >= 0
    flags = jnp.broadcast_to(on.astype(jnp.float32), (8, tokens)).astype(jnp.bfloat16)
    src = lax.broadcasted_iota(jnp.int32, (tokens, tokens), 0)
    dst = lax.broadcasted_iota(jnp.int32, (tokens, tokens), 1)
    upto = (src <= dst).astype(jnp.float32).astype(jnp.bfloat16)
    rank = jnp.dot(flags, upto, preferred_element_type=jnp.float32)[0:1, :].astype(jnp.int32)
    return jnp.where(on, rank, 0)


def project_kernel(chunk_start, own_ref, shard_ref, lab_hbm, seg_hbm, hid_hbm, w_hbm, mine_ref, theirs_ref, meta_ref, *rest):
    out_refs, (lab_ref, seg_ref, hid_ref, few_ref, acc_ref, small_sem, hid_sem, w_sem) = rest[:-8], rest[-8:]
    tokens, depth = hid_ref.shape
    rows = few_ref.shape[0]
    block = out_refs[0].shape[0]
    part = depth // hid_sem.shape[0]
    spans = [pl.ds(n, part) for n in range(0, depth, part)]
    count, chunk, _ = mine_ref.shape
    targets = [(theirs_ref, 1, n) for n in range(count)] + [(mine_ref, 0, n) for n in range(count)]
    starts = [chunk_start(shard_ref[0], slot, n) for _, slot, n in targets]
    small = [
        pltpu.make_async_copy(lab_hbm, lab_ref, small_sem.at[0]),
        pltpu.make_async_copy(seg_hbm, seg_ref, small_sem.at[1]),
    ]
    hid_copies = [
        pltpu.make_async_copy(hid_hbm.at[0, :, span], hid_ref.at[:, span], hid_sem.at[n])
        for n, span in enumerate(spans)
    ]
    w_copies = [
        pltpu.make_async_copy(w_hbm.at[0, pl.ds(start, chunk), :], ref.at[n], w_sem.at[m])
        for m, (start, (ref, _, n)) in enumerate(zip(starts, targets))
    ]
    queue = small + hid_copies + w_copies
    for copy in queue[: 2 + IN_FLIGHT]:
        copy.start()
    queue = queue[2 + IN_FLIGHT :]
    for copy in small:
        copy.wait()

    lab = lab_ref[...]
    seg = seg_ref[...]
    rank = ranks_along(lab)
    pick = rank == wanted_ranks(0, rows, own_ref[0], block)
    picker = pick.astype(jnp.float32).astype(jnp.bfloat16)
    for copy, span in zip(hid_copies, spans):
        copy.wait()
        if queue:
            queue.pop(0).start()
        few = jnp.dot(picker, hid_ref[:, span], preferred_element_type=jnp.float32)
        few_ref[:, span] = few.astype(jnp.bfloat16)

    mine = pick[:block, :]
    label = jnp.sum(jnp.where(mine, lab, 0).astype(jnp.float32), axis=1, keepdims=True)
    doc = jnp.sum(jnp.where(mine, seg, 0).astype(jnp.float32), axis=1, keepdims=True)
    same = (lab >= 0) & (seg.astype(jnp.float32) == doc)
    count = jnp.sum(jnp.where(same, 1.0, 0.0), axis=1, keepdims=True)
    weight = float(tokens) / (SEGS * jnp.maximum(count, 1.0))
    lane = lane_ids(block)
    meta_ref[...] = jnp.where(lane == 0, label, jnp.where(lane == 1, weight, 0.0))

    for m, (copy, start, (ref, _, n)) in enumerate(zip(w_copies, starts, targets)):
        copy.wait()
        if queue:
            queue.pop(0).start()
        term = jnp.dot(few_ref[:, pl.ds(start, chunk)], ref[n], preferred_element_type=jnp.float32)
        if m == 0:
            acc_ref[...] = term
        elif m < len(targets) - 1:
            acc_ref[...] += term
        else:
            logits = (acc_ref[...] + term).astype(jnp.bfloat16)
            for k, out_ref in enumerate(out_refs):
                out_ref[...] = logits[k * block : (k + 1) * block, :]


def project(ids, labels, segments, hidden, head_weight, peers, chunk_start, count):
    tokens, depth = hidden.shape[1:]
    width = head_weight.shape[2]
    rows = tokens - IGNORED
    block = rows // peers
    hbm = pl.BlockSpec(memory_space=pltpu.HBM)
    vmem = pl.BlockSpec(memory_space=pltpu.VMEM)
    return pl.pallas_call(
        functools.partial(project_kernel, chunk_start),
        in_specs=[pl.BlockSpec(memory_space=pltpu.SMEM)] * 2 + [hbm] * 4,
        out_specs=[vmem] * (3 + peers),
        out_shape=[jax.ShapeDtypeStruct((count, depth // (2 * count), width), jnp.bfloat16)] * 2
        + [jax.ShapeDtypeStruct((block, LANES), jnp.float32)]
        + [jax.ShapeDtypeStruct((block, width), jnp.bfloat16)] * peers,
        scratch_shapes=[
            pltpu.VMEM((1, tokens), jnp.int32),
            pltpu.VMEM((1, tokens), jnp.int32),
            pltpu.VMEM((tokens, depth), jnp.bfloat16),
            pltpu.VMEM((rows, depth), jnp.bfloat16),
            pltpu.VMEM((rows, width), jnp.float32),
            pltpu.SemaphoreType.DMA((2,)),
            pltpu.SemaphoreType.DMA((2,)),
            pltpu.SemaphoreType.DMA((2 * count,)),
        ],
        compiler_params=LARGE,
        cost_estimate=pl.CostEstimate(
            flops=2 * rows * depth * (width + tokens), bytes_accessed=0, transcendentals=0
        ),
        name="project",
    )(*ids, labels, segments, hidden, head_weight)


def pair_list(peers):
    return [(i, j) for i in range(peers) for j in range(peers) if i != j]


def stat_slots(peers):
    pairs = pair_list(peers)
    return peers, {p: peers + n for n, p in enumerate(pairs)}, peers + len(pairs)


def stats_kernel(own_ref, shard_ref, meta_ref, *refs):
    logit_refs, out_ref = refs[:-1], refs[-1]
    peers = len(logit_refs)
    block, width = logit_refs[0].shape
    _, pair_slot, target_slot = stat_slots(peers)
    span = LANES * GROUP // block
    lane = lane_ids(GROUP)
    sums = jnp.zeros((GROUP, LANES), jnp.float32)
    peaks = jnp.zeros((GROUP, LANES), jnp.float32)
    for g in range(block // GROUP):
        rows = slice(g * GROUP, (g + 1) * GROUP)
        label = meta_ref[rows, 0:1].astype(jnp.int32) - shard_ref[0] * width
        peak = []
        for ref in logit_refs:
            top = ref[rows, 0:LANES].astype(jnp.float32)
            for c in range(LANES, width, LANES):
                top = jnp.maximum(top, ref[rows, c : c + LANES].astype(jnp.float32))
            peak.append(jnp.max(top, axis=1, keepdims=True))
        total = [jnp.zeros((GROUP, LANES), jnp.float32) for _ in range(peers)]
        target = [jnp.zeros((GROUP, LANES), jnp.float32) for _ in range(peers)]
        cross = {p: jnp.zeros((GROUP, LANES), jnp.float32) for p in pair_slot}
        for c in range(0, width, LANES):
            l = [ref[rows, c : c + LANES].astype(jnp.float32) for ref in logit_refs]
            e = [jnp.exp(l[k] - peak[k]) for k in range(peers)]
            hit = (lane + c) == label
            for i in range(peers):
                total[i] += e[i]
                target[i] += jnp.where(hit, l[i], 0.0)
                for j in range(i + 1, peers):
                    gap = l[i] - l[j]
                    cross[i, j] += e[i] * gap
                    cross[j, i] -= e[j] * gap

        def put(slot, vals, top):
            nonlocal sums, peaks
            here = lane == g * span + slot
            sums = jnp.where(here, jnp.sum(vals, axis=1, keepdims=True), sums)
            if top is not None:
                peaks = jnp.where(here, top, peaks)

        for i in range(peers):
            put(i, total[i], peak[i])
            put(target_slot + i, target[i], None)
        for (i, j), slot in pair_slot.items():
            put(slot, cross[i, j], peak[i])
    out_ref[0:GROUP, :] = sums
    out_ref[GROUP : 2 * GROUP, :] = peaks


def stats(ids, meta, logits):
    block, width = logits[0].shape
    peers = len(logits)
    return pl.pallas_call(
        stats_kernel,
        in_specs=[pl.BlockSpec(memory_space=pltpu.SMEM)] * 2 + [pl.BlockSpec(memory_space=pltpu.VMEM)] * (1 + peers),
        out_shape=jax.ShapeDtypeStruct((2 * GROUP, LANES), jnp.float32),
        compiler_params=SMALL,
        cost_estimate=pl.CostEstimate(
            flops=40 * block * width * peers, bytes_accessed=2 * block * width * peers, transcendentals=block * width * peers
        ),
        name="stats",
    )(*ids, meta, *logits)


def merged(parts):
    top = parts[0][GROUP:, :]
    for part in parts[1:]:
        top = jnp.maximum(top, part[GROUP:, :])
    total = jnp.zeros_like(top)
    for part in parts:
        total += part[:GROUP, :] * jnp.exp(part[GROUP:, :] - top)
    return total, top


def merge_kernel(*refs):
    total, top = merged([ref[...] for ref in refs[:-1]])
    refs[-1][:GROUP, :] = total
    refs[-1][GROUP:, :] = top


def merge(parts):
    return pl.pallas_call(
        merge_kernel,
        in_specs=[pl.BlockSpec(memory_space=pltpu.VMEM)] * len(parts),
        out_shape=jax.ShapeDtypeStruct(parts[0].shape, jnp.float32),
        compiler_params=SMALL,
        name="merge",
    )(*parts)


def grad_kernel(count, own_ref, shard_ref, meta_ref, *refs):
    stat_refs, refs = refs[:count], refs[count:]
    peers = len(refs) // 2
    logit_refs, grad_refs = refs[:peers], refs[peers:]
    block, width = logit_refs[0].shape
    _, pair_slot, target_slot = stat_slots(peers)
    span = LANES * GROUP // block
    lane = lane_ids(GROUP)
    total, top = merged([ref[...] for ref in stat_refs])
    norm = top + jnp.log(jnp.maximum(total, 1e-37))
    third = 1.0 / (peers - 1)
    for g in range(block // GROUP):
        rows = slice(g * GROUP, (g + 1) * GROUP)
        at = lambda array, slot: array[:, g * span + slot : g * span + slot + 1]
        label = meta_ref[rows, 0:1].astype(jnp.int32) - shard_ref[0] * width
        weight = meta_ref[rows, 1:2]
        inverse = [1.0 / at(total, i) for i in range(peers)]
        norms = [at(norm, i) for i in range(peers)]
        mean = {p: at(total, slot) * inverse[p[0]] for p, slot in pair_slot.items()}
        shift = []
        for i in range(peers):
            ahead = sum(mean[i, j] for j in range(peers) if j != i)
            back = sum(mean[j, i] for j in range(peers) if j != i)
            loss = norms[i] - at(total, target_slot + i) + (ahead + back) * third
            terms = jnp.zeros((GROUP, LANES), jnp.float32)
            for n in range(LOSS_TERMS):
                term = loss.astype(jnp.bfloat16).astype(jnp.float32)
                loss = loss - term
                terms = jnp.where(lane == n, term, terms)
            grad_refs[i][rows, width:] = terms.astype(jnp.bfloat16)
            shift.append(1.0 + (peers - ahead) * third)
        for c in range(0, width, LANES):
            l = [ref[rows, c : c + LANES].astype(jnp.float32) for ref in logit_refs]
            p = [jnp.exp(l[k] - norms[k]) for k in range(peers)]
            common = sum(l) * third
            rest = sum(p) * third + jnp.where((lane + c) == label, 1.0, 0.0)
            for i in range(peers):
                grad = p[i] * (shift[i] + (l[i] * (peers * third) - common)) - rest
                grad_refs[i][rows, c : c + LANES] = (weight * grad).astype(jnp.bfloat16)


def gradients(ids, meta, parts, logits):
    block, width = logits[0].shape
    peers = len(logits)
    return pl.pallas_call(
        functools.partial(grad_kernel, len(parts)),
        in_specs=[pl.BlockSpec(memory_space=pltpu.SMEM)] * 2
        + [pl.BlockSpec(memory_space=pltpu.VMEM)] * (1 + len(parts) + peers),
        out_shape=[jax.ShapeDtypeStruct((block, width + LANES), jnp.bfloat16)] * peers,
        compiler_params=SMALL,
        cost_estimate=pl.CostEstimate(
            flops=20 * block * width * peers, bytes_accessed=4 * block * width * peers, transcendentals=block * width * peers
        ),
        name="gradients",
    )(*ids, meta, *parts, *logits)


def share_of(w_ref, index, grad):
    return lax.dot_general(w_ref[index], grad, (((1,), (1,)), ((), ())), preferred_element_type=jnp.float32)


def both_shares(mask, shard_ref, refs):
    mine_ref, theirs_ref, own_ref, other_ref = refs
    index = (shard_ref[0] // 2) ^ mask
    return share_of(mine_ref, index, own_ref[...]) + share_of(theirs_ref, index, other_ref[...])


def gather_kernel(peers, own_ref, shard_ref, *refs):
    block_refs, (own_all, other_all, loss_ref) = refs[:-3], refs[-3:]
    block, width = block_refs[0].shape[0], own_all.shape[1]
    for k in range(peers):
        rows = slice(k * block, (k + 1) * block)
        own_all[rows, :] = block_refs[k][:, :width]
        other_all[rows, :] = block_refs[peers + k][:, :width]
        loss_ref[rows, :] = jnp.sum(block_refs[k][:, width:].astype(jnp.float32), axis=1, keepdims=True)


def vmem_call(kernel, outs, cost, name, ids, *arrays):
    return pl.pallas_call(
        kernel,
        in_specs=[pl.BlockSpec(memory_space=pltpu.SMEM)] * 2 + [pl.BlockSpec(memory_space=pltpu.VMEM)] * len(arrays),
        out_specs=[pl.BlockSpec(memory_space=pltpu.VMEM)] * len(outs),
        out_shape=[jax.ShapeDtypeStruct(shape, dtype) for shape, dtype in outs],
        compiler_params=SMALL,
        cost_estimate=cost,
        name=name,
    )(*ids, *arrays)


def coded(value):
    depth, rows = value.shape
    top = jnp.maximum(jnp.max(jnp.abs(value), axis=0, keepdims=True), 1e-30)
    code = jnp.ceil(jnp.log2(top) * CODE_STEPS)
    unit = jnp.exp2(code * (-1.0 / CODE_STEPS)) * CODE_TOP
    whole = jnp.clip(jnp.round(value * unit), -CODE_TOP - 1, CODE_TOP + 1)
    codes = jnp.broadcast_to(code, (CODE_ROWS, rows))
    return whole.astype(jnp.int32).astype(jnp.int16), codes.astype(jnp.int32).astype(jnp.int16)


def put_coded(ref, value):
    depth = value.shape[0]
    ref[:depth, :], ref[depth:, :] = coded(value)


def get_coded(ref):
    depth = ref.shape[0] - CODE_ROWS
    code = ref[depth:, :].astype(jnp.int32).astype(jnp.float32)[0:1, :]
    unit = jnp.exp2(code * (1.0 / CODE_STEPS)) * (1.0 / CODE_TOP)
    return ref[:depth, :].astype(jnp.int32).astype(jnp.float32) * unit


def encode_kernel(mask, own_ref, shard_ref, *refs):
    put_coded(refs[4], both_shares(mask, shard_ref, refs[:4]))


def is_middle(shard_ref):
    chip = shard_ref[0] // 2
    return (chip == 1) | (chip == 2)


def relay_kernel(own_ref, shard_ref, value_ref, coded_ref, out_ref):
    put_coded(out_ref, value_ref[...] + jnp.where(is_middle(shard_ref), get_coded(coded_ref), 0.0))


def sum_kernel(mask, own_ref, shard_ref, *refs):
    refs[-1][...] = both_shares(mask, shard_ref, refs[:4])


def keep_kernel(own_ref, shard_ref, *refs):
    value = both_shares(0, shard_ref, refs[:4])
    for ref in refs[4:-1]:
        value += jnp.where(is_middle(shard_ref), 0.0, get_coded(ref))
    refs[-1][...] = value


def place_kernel(peers, own_ref, shard_ref, row_ref, loss_ref, place_ref, out_ref):
    tokens, rows = place_ref.shape
    block = rows // peers
    rank = ranks_along(row_ref[...])
    here = rank == wanted_ranks(0, rows, own_ref[0], block)
    out_ref[...] = jnp.sum(jnp.where(here, loss_ref[...], 0.0), axis=0, keepdims=True)

    src = lax.broadcasted_iota(jnp.int32, (tokens, tokens), 0)
    dst = lax.broadcasted_iota(jnp.int32, (tokens, tokens), 1)
    flags = (row_ref[...] >= 0).astype(jnp.float32).astype(jnp.bfloat16)
    flags = jnp.broadcast_to(flags, (LANES, tokens))
    turned = lambda keep: lax.dot_general(
        keep.astype(jnp.float32).astype(jnp.bfloat16),
        flags,
        (((1,), (1,)), ((), ())),
        preferred_element_type=jnp.float32,
    )[:, 0:1]
    rank = (turned(dst <= src) * turned(dst == src)).astype(jnp.int32)
    col = lax.broadcasted_iota(jnp.int32, (1, rows), 1)
    wanted = (own_ref[0] ^ (col // block)) * block + col % block + 1
    place_ref[...] = (rank == wanted).astype(jnp.float32).astype(jnp.bfloat16)


def place(ids, labels, losses, peers):
    tokens = labels.shape[1]
    return vmem_call(
        functools.partial(place_kernel, peers),
        [((tokens, tokens - IGNORED), jnp.bfloat16), ((1, tokens), jnp.float32)],
        pl.CostEstimate(flops=4 * tokens * tokens * LANES, bytes_accessed=0, transcendentals=0),
        "place",
        ids,
        labels,
        losses,
    )


def finish_kernel(place_ref, sum_ref, *refs):
    coded_refs, (out_hbm, out_ref, sems) = refs[:-3], refs[-3:]
    value = sum_ref[...]
    for ref in coded_refs:
        value += get_coded(ref)
    high = value.astype(jnp.bfloat16)
    low = (value - high.astype(jnp.float32)).astype(jnp.bfloat16)
    turned = lambda place, piece: lax.dot_general(
        place, piece, (((1,), (1,)), ((), ())), preferred_element_type=jnp.float32
    )
    part = out_ref.shape[0] // sems.shape[0]
    copies = []
    for n in range(sems.shape[0]):
        span = pl.ds(n * part, part)
        place = place_ref[span, :]
        out_ref[span, :] = turned(place, high) + turned(place, low)
        copies.append(pltpu.make_async_copy(out_ref.at[span, :], out_hbm.at[0, span, :], sems.at[n]))
        copies[-1].start()
    for copy in copies:
        copy.wait()


def finish(placing, kept, arrived):
    tokens, rows = placing.shape
    depth = kept.shape[0]
    return pl.pallas_call(
        finish_kernel,
        in_specs=[pl.BlockSpec(memory_space=pltpu.VMEM)] * (2 + len(arrived)),
        out_specs=pl.BlockSpec(memory_space=pltpu.HBM),
        out_shape=jax.ShapeDtypeStruct((1, tokens, depth), jnp.float32),
        scratch_shapes=[pltpu.VMEM((tokens, depth), jnp.float32), pltpu.SemaphoreType.DMA((4,))],
        compiler_params=SMALL,
        cost_estimate=pl.CostEstimate(flops=1000, bytes_accessed=0, transcendentals=0),
        name="finish",
    )(placing, kept, *arrived)


def swap(array, axis, size, mask):
    return lax.ppermute(array, axis, [(i, i ^ mask) for i in range(size)])


def hop(array, pairs):
    return lax.ppermute(array, "vocab", [(2 * a + c, 2 * b + c) for a, b in pairs for c in range(2)])


def on_device(hidden, head_weight, labels, segments):
    peers = lax.axis_size("peer")
    shards = lax.axis_size("vocab")
    width = head_weight.shape[2]
    depth = head_weight.shape[1] // shards
    tokens = labels.shape[0]
    rows = tokens - IGNORED
    chips = shards // 2
    labels, segments = labels[None, :], segments[None, :]
    ids = [lax.axis_index(name).astype(jnp.int32).reshape(1) for name in ("peer", "vocab")]
    by_core = depth % LANES == 0

    def chunk_start(shard, slot, n):
        if by_core:
            return pl.multiple_of((2 * n + ((shard % 2) ^ slot)) * depth, depth)
        return (n + slot * PLAIN_CHUNKS) * (head_weight.shape[1] // (2 * PLAIN_CHUNKS))

    in_hbm = [pltpu.with_memory_space_constraint(x, pltpu.HBM) for x in (labels, segments, hidden, head_weight)]
    w_mine, w_theirs, meta, *blocks = project(
        ids, *in_hbm, peers, chunk_start, chips if by_core else PLAIN_CHUNKS
    )

    def across(arrays):
        moved = {k: swap(arrays[k], "peer", peers, k) for k in range(peers - 1, 0, -1)}
        return [arrays[0]] + [moved[k] for k in range(1, peers)]

    core_swap = lambda array: swap(array, "vocab", shards, 1)
    logits = across(blocks)
    part = stats(ids, meta, logits)
    part = merge([part, core_swap(part)])
    after = lambda array, *before: lax.optimization_barrier((array,) + before)[0]
    w_given = core_swap(after(w_theirs, part)) if by_core else None
    parts = [part] + [swap(part, "vocab", shards, 2 * mask) for mask in range(chips - 1, 0, -1)]
    grads = across(gradients(ids, meta, parts, logits))

    cost = pl.CostEstimate(flops=1000, bytes_accessed=0, transcendentals=0)
    flat = ((rows, width), jnp.bfloat16)
    kernel = functools.partial(gather_kernel, peers)
    outs = [flat, flat, ((rows, 1), jnp.float32)]
    others = [core_swap(grad) for grad in grads]
    own_grad, other_grad, losses = vmem_call(kernel, outs, cost, "gather", ids, *grads, *others)
    placing, token_loss = place(ids, labels, losses, peers)
    if by_core:
        operands = (w_mine, w_given, own_grad, other_grad)
        coded_shape, full = ((depth + CODE_ROWS, rows), jnp.int16), ((depth, rows), jnp.float32)

        def encode(mask, *more):
            kernel = functools.partial(encode_kernel, mask)
            return vmem_call(kernel, [coded_shape, *more], cost, "encode", ids, *operands)

        if chips == 4:
            (two,) = encode(2)
            first = hop(two, [(0, 1), (3, 2), (1, 3), (2, 0)])
            kernel = functools.partial(sum_kernel, 3)
            (three,) = vmem_call(kernel, [full], cost, "share", ids, *operands)
            (one,) = encode(1)
            (relayed,) = vmem_call(relay_kernel, [coded_shape], cost, "relay", ids, three, first)
            cross = swap(relayed, "vocab", shards, 6)
            near = swap(one, "vocab", shards, 2)
            early, arrived = [first], [cross, near]
        else:
            early = []
            arrived = [swap(encode(mask)[0], "vocab", shards, 2 * mask) for mask in range(chips - 1, 0, -1)]
        (kept,) = vmem_call(keep_kernel, [((depth, rows), jnp.float32)], cost, "keep", ids, *operands, *early)
    else:
        arrived = []
        share = lax.dot_general(
            head_weight[0], own_grad, (((1,), (1,)), ((), ())), preferred_element_type=jnp.float32
        )
        kept = lax.psum_scatter(share, "vocab", scatter_dimension=0, tiled=True)
    grad_hidden = finish(placing, kept, arrived)
    return grad_hidden, token_loss


def solution(mesh):
    in_specs = (P("peer", None, None), P("peer", None, "vocab"), P(), P())
    out_specs = (P("peer", None, "vocab"), P("peer", None))
    return jax.shard_map(on_device, mesh=mesh, in_specs=in_specs, out_specs=out_specs, check_vma=False)
```

```python
import functools
import jax
import jax.numpy as jnp
from jax import lax
from jax.experimental import pallas as pl
from jax.experimental.pallas import tpu as pltpu
from jax.sharding import PartitionSpec as P

SEGS = 8
IGNORED = 256
GROUP = 16
LANES = 128
PLAIN_CHUNKS = 4
IN_FLIGHT = 4
LOSS_TERMS = 3
CODE_ROWS = 16
CODE_STEPS = 64.0
CODE_TOP = 32766.0
LARGE = pltpu.CompilerParams(vmem_limit_bytes=32 * 1024 * 1024)
SMALL = pltpu.CompilerParams(vmem_limit_bytes=16 * 1024 * 1024)


def lane_ids(rows):
    return lax.broadcasted_iota(jnp.int32, (rows, LANES), 1)


def wanted_ranks(first, count, own, block):
    row = lax.broadcasted_iota(jnp.int32, (count, 1), 0) + first
    return (own ^ (row // block)) * block + row % block + 1


def ranks_along(labels):
    tokens = labels.shape[1]
    on = labels >= 0
    flags = jnp.broadcast_to(on.astype(jnp.float32), (8, tokens)).astype(jnp.bfloat16)
    src = lax.broadcasted_iota(jnp.int32, (tokens, tokens), 0)
    dst = lax.broadcasted_iota(jnp.int32, (tokens, tokens), 1)
    upto = (src <= dst).astype(jnp.float32).astype(jnp.bfloat16)
    rank = jnp.dot(flags, upto, preferred_element_type=jnp.float32)[0:1, :].astype(jnp.int32)
    return jnp.where(on, rank, 0)


def project_kernel(chunk_start, own_ref, shard_ref, lab_hbm, seg_hbm, hid_hbm, w_hbm, mine_ref, theirs_ref, meta_ref, *rest):
    out_refs, (lab_ref, seg_ref, hid_ref, few_ref, acc_ref, small_sem, hid_sem, w_sem) = rest[:-8], rest[-8:]
    tokens, depth = hid_ref.shape
    rows = few_ref.shape[0]
    block = out_refs[0].shape[0]
    part = depth // hid_sem.shape[0]
    spans = [pl.ds(n, part) for n in range(0, depth, part)]
    count, chunk, _ = mine_ref.shape
    targets = [(theirs_ref, 1, n) for n in range(count)] + [(mine_ref, 0, n) for n in range(count)]
    starts = [chunk_start(shard_ref[0], slot, n) for _, slot, n in targets]
    small = [
        pltpu.make_async_copy(lab_hbm, lab_ref, small_sem.at[0]),
        pltpu.make_async_copy(seg_hbm, seg_ref, small_sem.at[1]),
    ]
    hid_copies = [
        pltpu.make_async_copy(hid_hbm.at[0, :, span], hid_ref.at[:, span], hid_sem.at[n])
        for n, span in enumerate(spans)
    ]
    w_copies = [
        pltpu.make_async_copy(w_hbm.at[0, pl.ds(start, chunk), :], ref.at[n], w_sem.at[m])
        for m, (start, (ref, _, n)) in enumerate(zip(starts, targets))
    ]
    queue = small + hid_copies + w_copies
    for copy in queue[: 2 + IN_FLIGHT]:
        copy.start()
    queue = queue[2 + IN_FLIGHT :]
    for copy in small:
        copy.wait()

    lab = lab_ref[...]
    seg = seg_ref[...]
    rank = ranks_along(lab)
    pick = rank == wanted_ranks(0, rows, own_ref[0], block)
    picker = pick.astype(jnp.float32).astype(jnp.bfloat16)
    for copy, span in zip(hid_copies, spans):
        copy.wait()
        if queue:
            queue.pop(0).start()
        few = jnp.dot(picker, hid_ref[:, span], preferred_element_type=jnp.float32)
        few_ref[:, span] = few.astype(jnp.bfloat16)

    mine = pick[:block, :]
    label = jnp.sum(jnp.where(mine, lab, 0).astype(jnp.float32), axis=1, keepdims=True)
    doc = jnp.sum(jnp.where(mine, seg, 0).astype(jnp.float32), axis=1, keepdims=True)
    same = (lab >= 0) & (seg.astype(jnp.float32) == doc)
    count = jnp.sum(jnp.where(same, 1.0, 0.0), axis=1, keepdims=True)
    weight = float(tokens) / (SEGS * jnp.maximum(count, 1.0))
    lane = lane_ids(block)
    meta_ref[...] = jnp.where(lane == 0, label, jnp.where(lane == 1, weight, 0.0))

    for m, (copy, start, (ref, _, n)) in enumerate(zip(w_copies, starts, targets)):
        copy.wait()
        if queue:
            queue.pop(0).start()
        term = jnp.dot(few_ref[:, pl.ds(start, chunk)], ref[n], preferred_element_type=jnp.float32)
        if m == 0:
            acc_ref[...] = term
        elif m < len(targets) - 1:
            acc_ref[...] += term
        else:
            logits = (acc_ref[...] + term).astype(jnp.bfloat16)
            for k, out_ref in enumerate(out_refs):
                out_ref[...] = logits[k * block : (k + 1) * block, :]


def project(ids, labels, segments, hidden, head_weight, peers, chunk_start, count):
    tokens, depth = hidden.shape[1:]
    width = head_weight.shape[2]
    rows = tokens - IGNORED
    block = rows // peers
    hbm = pl.BlockSpec(memory_space=pltpu.HBM)
    vmem = pl.BlockSpec(memory_space=pltpu.VMEM)
    return pl.pallas_call(
        functools.partial(project_kernel, chunk_start),
        in_specs=[pl.BlockSpec(memory_space=pltpu.SMEM)] * 2 + [hbm] * 4,
        out_specs=[vmem] * (3 + peers),
        out_shape=[jax.ShapeDtypeStruct((count, depth // (2 * count), width), jnp.bfloat16)] * 2
        + [jax.ShapeDtypeStruct((block, LANES), jnp.float32)]
        + [jax.ShapeDtypeStruct((block, width), jnp.bfloat16)] * peers,
        scratch_shapes=[
            pltpu.VMEM((1, tokens), jnp.int32),
            pltpu.VMEM((1, tokens), jnp.int32),
            pltpu.VMEM((tokens, depth), jnp.bfloat16),
            pltpu.VMEM((rows, depth), jnp.bfloat16),
            pltpu.VMEM((rows, width), jnp.float32),
            pltpu.SemaphoreType.DMA((2,)),
            pltpu.SemaphoreType.DMA((2,)),
            pltpu.SemaphoreType.DMA((2 * count,)),
        ],
        compiler_params=LARGE,
        cost_estimate=pl.CostEstimate(
            flops=2 * rows * depth * (width + tokens), bytes_accessed=0, transcendentals=0
        ),
        name="project",
    )(*ids, labels, segments, hidden, head_weight)


def pair_list(peers):
    return [(i, j) for i in range(peers) for j in range(peers) if i != j]


def stat_slots(peers):
    pairs = pair_list(peers)
    return peers, {p: peers + n for n, p in enumerate(pairs)}, peers + len(pairs)


def stats_kernel(own_ref, shard_ref, meta_ref, *refs):
    logit_refs, out_ref = refs[:-1], refs[-1]
    peers = len(logit_refs)
    block, width = logit_refs[0].shape
    _, pair_slot, target_slot = stat_slots(peers)
    span = LANES * GROUP // block
    lane = lane_ids(GROUP)
    sums = jnp.zeros((GROUP, LANES), jnp.float32)
    peaks = jnp.zeros((GROUP, LANES), jnp.float32)
    for g in range(block // GROUP):
        rows = slice(g * GROUP, (g + 1) * GROUP)
        label = meta_ref[rows, 0:1].astype(jnp.int32) - shard_ref[0] * width
        peak = []
        for ref in logit_refs:
            top = ref[rows, 0:LANES].astype(jnp.float32)
            for c in range(LANES, width, LANES):
                top = jnp.maximum(top, ref[rows, c : c + LANES].astype(jnp.float32))
            peak.append(jnp.max(top, axis=1, keepdims=True))
        total = [jnp.zeros((GROUP, LANES), jnp.float32) for _ in range(peers)]
        target = [jnp.zeros((GROUP, LANES), jnp.float32) for _ in range(peers)]
        cross = {p: jnp.zeros((GROUP, LANES), jnp.float32) for p in pair_slot}
        for c in range(0, width, LANES):
            l = [ref[rows, c : c + LANES].astype(jnp.float32) for ref in logit_refs]
            e = [jnp.exp(l[k] - peak[k]) for k in range(peers)]
            hit = (lane + c) == label
            for i in range(peers):
                total[i] += e[i]
                target[i] += jnp.where(hit, l[i], 0.0)
                for j in range(i + 1, peers):
                    gap = l[i] - l[j]
                    cross[i, j] += e[i] * gap
                    cross[j, i] -= e[j] * gap

        def put(slot, vals, top):
            nonlocal sums, peaks
            here = lane == g * span + slot
            sums = jnp.where(here, jnp.sum(vals, axis=1, keepdims=True), sums)
            if top is not None:
                peaks = jnp.where(here, top, peaks)

        for i in range(peers):
            put(i, total[i], peak[i])
            put(target_slot + i, target[i], None)
        for (i, j), slot in pair_slot.items():
            put(slot, cross[i, j], peak[i])
    out_ref[0:GROUP, :] = sums
    out_ref[GROUP : 2 * GROUP, :] = peaks


def stats(ids, meta, logits):
    block, width = logits[0].shape
    peers = len(logits)
    return pl.pallas_call(
        stats_kernel,
        in_specs=[pl.BlockSpec(memory_space=pltpu.SMEM)] * 2 + [pl.BlockSpec(memory_space=pltpu.VMEM)] * (1 + peers),
        out_shape=jax.ShapeDtypeStruct((2 * GROUP, LANES), jnp.float32),
        compiler_params=SMALL,
        cost_estimate=pl.CostEstimate(
            flops=40 * block * width * peers, bytes_accessed=2 * block * width * peers, transcendentals=block * width * peers
        ),
        name="stats",
    )(*ids, meta, *logits)


def merged(parts):
    top = parts[0][GROUP:, :]
    for part in parts[1:]:
        top = jnp.maximum(top, part[GROUP:, :])
    total = jnp.zeros_like(top)
    for part in parts:
        total += part[:GROUP, :] * jnp.exp(part[GROUP:, :] - top)
    return total, top


def merge_kernel(*refs):
    total, top = merged([ref[...] for ref in refs[:-1]])
    refs[-1][:GROUP, :] = total
    refs[-1][GROUP:, :] = top


def merge(parts):
    return pl.pallas_call(
        merge_kernel,
        in_specs=[pl.BlockSpec(memory_space=pltpu.VMEM)] * len(parts),
        out_shape=jax.ShapeDtypeStruct(parts[0].shape, jnp.float32),
        compiler_params=SMALL,
        name="merge",
    )(*parts)


def grad_kernel(count, own_ref, shard_ref, meta_ref, *refs):
    stat_refs, refs = refs[:count], refs[count:]
    peers = len(refs) // 3
    logit_refs, grad_refs, loss_refs = refs[:peers], refs[peers : 2 * peers], refs[2 * peers :]
    block, width = logit_refs[0].shape
    _, pair_slot, target_slot = stat_slots(peers)
    span = LANES * GROUP // block
    lane = lane_ids(GROUP)
    total, top = merged([ref[...] for ref in stat_refs])
    norm = top + jnp.log(jnp.maximum(total, 1e-37))
    third = 1.0 / (peers - 1)
    for g in range(block // GROUP):
        rows = slice(g * GROUP, (g + 1) * GROUP)
        at = lambda array, slot: array[:, g * span + slot : g * span + slot + 1]
        label = meta_ref[rows, 0:1].astype(jnp.int32) - shard_ref[0] * width
        weight = meta_ref[rows, 1:2]
        inverse = [1.0 / at(total, i) for i in range(peers)]
        norms = [at(norm, i) for i in range(peers)]
        mean = {p: at(total, slot) * inverse[p[0]] for p, slot in pair_slot.items()}
        shift = []
        for i in range(peers):
            ahead = sum(mean[i, j] for j in range(peers) if j != i)
            back = sum(mean[j, i] for j in range(peers) if j != i)
            loss = norms[i] - at(total, target_slot + i) + (ahead + back) * third
            loss_refs[i][rows, :] = jnp.broadcast_to(loss, (GROUP, LANES))
            shift.append(1.0 + (peers - ahead) * third)
        for c in range(0, width, LANES):
            l = [ref[rows, c : c + LANES].astype(jnp.float32) for ref in logit_refs]
            p = [jnp.exp(l[k] - norms[k]) for k in range(peers)]
            common = sum(l) * third
            rest = sum(p) * third + jnp.where((lane + c) == label, 1.0, 0.0)
            for i in range(peers):
                grad = p[i] * (shift[i] + (l[i] * (peers * third) - common)) - rest
                grad_refs[i][rows, c : c + LANES] = (weight * grad).astype(jnp.bfloat16)


def gradients(ids, meta, parts, logits):
    block, width = logits[0].shape
    peers = len(logits)
    return pl.pallas_call(
        functools.partial(grad_kernel, len(parts)),
        in_specs=[pl.BlockSpec(memory_space=pltpu.SMEM)] * 2
        + [pl.BlockSpec(memory_space=pltpu.VMEM)] * (1 + len(parts) + peers),
        out_shape=[jax.ShapeDtypeStruct((block, width), jnp.bfloat16)] * peers
        + [jax.ShapeDtypeStruct((block, LANES), jnp.float32)] * peers,
        compiler_params=SMALL,
        cost_estimate=pl.CostEstimate(
            flops=20 * block * width * peers, bytes_accessed=4 * block * width * peers, transcendentals=block * width * peers
        ),
        name="gradients",
    )(*ids, meta, *parts, *logits)


def share_of(w_ref, index, grad):
    return lax.dot_general(w_ref[index], grad, (((1,), (1,)), ((), ())), preferred_element_type=jnp.float32)


def both_shares(mask, shard_ref, refs):
    mine_ref, theirs_ref, own_ref, other_ref = refs
    index = (shard_ref[0] // 2) ^ mask
    return share_of(mine_ref, index, own_ref[...]) + share_of(theirs_ref, index, other_ref[...])


def gather_kernel(peers, own_ref, shard_ref, *refs):
    block_refs, (own_all, other_all) = refs[:-2], refs[-2:]
    block, width = block_refs[0].shape[0], own_all.shape[1]
    for k in range(peers):
        rows = slice(k * block, (k + 1) * block)
        own_all[rows, :] = block_refs[k][:, :width]
        other_all[rows, :] = block_refs[peers + k][:, :width]


def vmem_call(kernel, outs, cost, name, ids, *arrays):
    return pl.pallas_call(
        kernel,
        in_specs=[pl.BlockSpec(memory_space=pltpu.SMEM)] * 2 + [pl.BlockSpec(memory_space=pltpu.VMEM)] * len(arrays),
        out_specs=[pl.BlockSpec(memory_space=pltpu.VMEM)] * len(outs),
        out_shape=[jax.ShapeDtypeStruct(shape, dtype) for shape, dtype in outs],
        compiler_params=SMALL,
        cost_estimate=cost,
        name=name,
    )(*ids, *arrays)


def coded(value):
    depth, rows = value.shape
    top = jnp.maximum(jnp.max(jnp.abs(value), axis=0, keepdims=True), 1e-30)
    code = jnp.ceil(jnp.log2(top) * CODE_STEPS)
    unit = jnp.exp2(code * (-1.0 / CODE_STEPS)) * CODE_TOP
    whole = jnp.clip(jnp.round(value * unit), -CODE_TOP - 1, CODE_TOP + 1)
    codes = jnp.broadcast_to(code, (CODE_ROWS, rows))
    return whole.astype(jnp.int32).astype(jnp.int16), codes.astype(jnp.int32).astype(jnp.int16)


def put_coded(ref, value):
    depth = value.shape[0]
    ref[:depth, :], ref[depth:, :] = coded(value)


def get_coded(ref):
    depth = ref.shape[0] - CODE_ROWS
    code = ref[depth:, :].astype(jnp.int32).astype(jnp.float32)[0:1, :]
    unit = jnp.exp2(code * (1.0 / CODE_STEPS)) * (1.0 / CODE_TOP)
    return ref[:depth, :].astype(jnp.int32).astype(jnp.float32) * unit


def encode_kernel(mask, own_ref, shard_ref, *refs):
    put_coded(refs[4], both_shares(mask, shard_ref, refs[:4]))


def is_middle(shard_ref):
    chip = shard_ref[0] // 2
    return (chip == 1) | (chip == 2)


def relay_kernel(own_ref, shard_ref, value_ref, coded_ref, out_ref):
    put_coded(out_ref, value_ref[...] + jnp.where(is_middle(shard_ref), get_coded(coded_ref), 0.0))


def sum_kernel(mask, own_ref, shard_ref, *refs):
    refs[-1][...] = both_shares(mask, shard_ref, refs[:4])


def keep_kernel(own_ref, shard_ref, *refs):
    value = both_shares(0, shard_ref, refs[:4])
    for ref in refs[4:-1]:
        value += jnp.where(is_middle(shard_ref), 0.0, get_coded(ref))
    refs[-1][...] = value


def place_kernel(peers, own_ref, shard_ref, row_ref, *refs):
    loss_refs, (place_ref, out_ref) = refs[:peers], refs[peers:]
    tokens, rows = place_ref.shape
    block = rows // peers
    rank = ranks_along(row_ref[...])
    here = rank == wanted_ranks(0, rows, own_ref[0], block)
    out_ref[...] = jnp.sum(jnp.where(here, jnp.concatenate([ref[:, 0:1] for ref in loss_refs], axis=0), 0.0), axis=0, keepdims=True)

    src = lax.broadcasted_iota(jnp.int32, (tokens, tokens), 0)
    dst = lax.broadcasted_iota(jnp.int32, (tokens, tokens), 1)
    flags = (row_ref[...] >= 0).astype(jnp.float32).astype(jnp.bfloat16)
    flags = jnp.broadcast_to(flags, (LANES, tokens))
    turned = lambda keep: lax.dot_general(
        keep.astype(jnp.float32).astype(jnp.bfloat16),
        flags,
        (((1,), (1,)), ((), ())),
        preferred_element_type=jnp.float32,
    )[:, 0:1]
    rank = (turned(dst <= src) * turned(dst == src)).astype(jnp.int32)
    col = lax.broadcasted_iota(jnp.int32, (1, rows), 1)
    wanted = (own_ref[0] ^ (col // block)) * block + col % block + 1
    place_ref[...] = (rank == wanted).astype(jnp.float32).astype(jnp.bfloat16)


def place(ids, labels, losses, peers):
    tokens = labels.shape[1]
    return vmem_call(
        functools.partial(place_kernel, peers),
        [((tokens, tokens - IGNORED), jnp.bfloat16), ((1, tokens), jnp.float32)],
        pl.CostEstimate(flops=4 * tokens * tokens * LANES, bytes_accessed=0, transcendentals=0),
        "place",
        ids,
        labels,
        *losses,
    )


def finish_kernel(place_ref, sum_ref, *refs):
    coded_refs, (out_hbm, out_ref, sems) = refs[:-3], refs[-3:]
    value = sum_ref[...]
    for ref in coded_refs:
        value += get_coded(ref)
    high = value.astype(jnp.bfloat16)
    low = (value - high.astype(jnp.float32)).astype(jnp.bfloat16)
    turned = lambda place, piece: lax.dot_general(
        place, piece, (((1,), (1,)), ((), ())), preferred_element_type=jnp.float32
    )
    part = out_ref.shape[0] // sems.shape[0]
    copies = []
    for n in range(sems.shape[0]):
        span = pl.ds(n * part, part)
        place = place_ref[span, :]
        out_ref[span, :] = turned(place, high) + turned(place, low)
        copies.append(pltpu.make_async_copy(out_ref.at[span, :], out_hbm.at[0, span, :], sems.at[n]))
        copies[-1].start()
    for copy in copies:
        copy.wait()


def finish(placing, kept, arrived):
    tokens, rows = placing.shape
    depth = kept.shape[0]
    return pl.pallas_call(
        finish_kernel,
        in_specs=[pl.BlockSpec(memory_space=pltpu.VMEM)] * (2 + len(arrived)),
        out_specs=pl.BlockSpec(memory_space=pltpu.HBM),
        out_shape=jax.ShapeDtypeStruct((1, tokens, depth), jnp.float32),
        scratch_shapes=[pltpu.VMEM((tokens, depth), jnp.float32), pltpu.SemaphoreType.DMA((4,))],
        compiler_params=SMALL,
        cost_estimate=pl.CostEstimate(flops=1000, bytes_accessed=0, transcendentals=0),
        name="finish",
    )(placing, kept, *arrived)


def swap(array, axis, size, mask):
    return lax.ppermute(array, axis, [(i, i ^ mask) for i in range(size)])


def hop(array, pairs):
    return lax.ppermute(array, "vocab", [(2 * a + c, 2 * b + c) for a, b in pairs for c in range(2)])


def on_device(hidden, head_weight, labels, segments):
    peers = lax.axis_size("peer")
    shards = lax.axis_size("vocab")
    width = head_weight.shape[2]
    depth = head_weight.shape[1] // shards
    tokens = labels.shape[0]
    rows = tokens - IGNORED
    chips = shards // 2
    labels, segments = labels[None, :], segments[None, :]
    ids = [lax.axis_index(name).astype(jnp.int32).reshape(1) for name in ("peer", "vocab")]
    by_core = depth % LANES == 0

    def chunk_start(shard, slot, n):
        if by_core:
            return pl.multiple_of((2 * n + ((shard % 2) ^ slot)) * depth, depth)
        return (n + slot * PLAIN_CHUNKS) * (head_weight.shape[1] // (2 * PLAIN_CHUNKS))

    in_hbm = [pltpu.with_memory_space_constraint(x, pltpu.HBM) for x in (labels, segments, hidden, head_weight)]
    w_mine, w_theirs, meta, *blocks = project(
        ids, *in_hbm, peers, chunk_start, chips if by_core else PLAIN_CHUNKS
    )

    def across(arrays):
        moved = {k: swap(arrays[k], "peer", peers, k) for k in range(peers - 1, 0, -1)}
        return [arrays[0]] + [moved[k] for k in range(1, peers)]

    core_swap = lambda array: swap(array, "vocab", shards, 1)
    logits = across(blocks)
    part = stats(ids, meta, logits)
    part = merge([part, core_swap(part)])
    after = lambda array, *before: lax.optimization_barrier((array,) + before)[0]
    w_given = core_swap(after(w_theirs, part)) if by_core else None
    parts = [part] + [swap(part, "vocab", shards, 2 * mask) for mask in range(chips - 1, 0, -1)]
    outs = gradients(ids, meta, parts, logits)
    grads, losses = across(outs[:peers]), outs[peers:]

    cost = pl.CostEstimate(flops=1000, bytes_accessed=0, transcendentals=0)
    flat = ((rows, width), jnp.bfloat16)
    kernel = functools.partial(gather_kernel, peers)
    outs = [flat, flat]
    others = [core_swap(grad) for grad in grads]
    own_grad, other_grad = vmem_call(kernel, outs, cost, "gather", ids, *grads, *others)
    if by_core:
        operands = (w_mine, w_given, own_grad, other_grad)
        coded_shape, full = ((depth + CODE_ROWS, rows), jnp.int16), ((depth, rows), jnp.float32)

        def encode(mask, *more):
            kernel = functools.partial(encode_kernel, mask)
            return vmem_call(kernel, [coded_shape, *more], cost, "encode", ids, *operands)

        if chips == 4:
            (two,) = encode(2)
            first = hop(two, [(0, 1), (3, 2), (1, 3), (2, 0)])
            kernel = functools.partial(sum_kernel, 3)
            (three,) = vmem_call(kernel, [full], cost, "share", ids, *operands)
            (one,) = encode(1)
            (relayed,) = vmem_call(relay_kernel, [coded_shape], cost, "relay", ids, three, first)
            cross = swap(relayed, "vocab", shards, 6)
            near = swap(one, "vocab", shards, 2)
            early, arrived = [first], [cross, near]
        else:
            early = []
            arrived = [swap(encode(mask)[0], "vocab", shards, 2 * mask) for mask in range(chips - 1, 0, -1)]
        (kept,) = vmem_call(keep_kernel, [((depth, rows), jnp.float32)], cost, "keep", ids, *operands, *early)
    else:
        arrived = []
        share = lax.dot_general(
            head_weight[0], own_grad, (((1,), (1,)), ((), ())), preferred_element_type=jnp.float32
        )
        kept = lax.psum_scatter(share, "vocab", scatter_dimension=0, tiled=True)
    losses = across([after(loss, kept) for loss in losses])
    placing, token_loss = place(ids, labels, losses, peers)
    grad_hidden = finish(placing, kept, arrived)
    return grad_hidden, token_loss


def solution(mesh):
    in_specs = (P("peer", None, None), P("peer", None, "vocab"), P(), P())
    out_specs = (P("peer", None, "vocab"), P("peer", None))
    return jax.shard_map(on_device, mesh=mesh, in_specs=in_specs, out_specs=out_specs, check_vma=False)
```

```python
import functools
import jax
import jax.numpy as jnp
from jax import lax
from jax.experimental import pallas as pl
from jax.experimental.pallas import tpu as pltpu
from jax.sharding import PartitionSpec as P

SEGS = 8
IGNORED = 256
GROUP = 16
LANES = 128
PLAIN_CHUNKS = 4
IN_FLIGHT = 4
LOSS_TERMS = 3
CODE_ROWS = 16
CODE_STEPS = 64.0
CODE_TOP = 32766.0
LARGE = pltpu.CompilerParams(vmem_limit_bytes=32 * 1024 * 1024)
SMALL = pltpu.CompilerParams(vmem_limit_bytes=16 * 1024 * 1024)


def lane_ids(rows):
    return lax.broadcasted_iota(jnp.int32, (rows, LANES), 1)


def wanted_ranks(first, count, own, block):
    row = lax.broadcasted_iota(jnp.int32, (count, 1), 0) + first
    return (own ^ (row // block)) * block + row % block + 1


def ranks_along(labels):
    tokens = labels.shape[1]
    on = labels >= 0
    flags = jnp.broadcast_to(on.astype(jnp.float32), (8, tokens)).astype(jnp.bfloat16)
    src = lax.broadcasted_iota(jnp.int32, (tokens, tokens), 0)
    dst = lax.broadcasted_iota(jnp.int32, (tokens, tokens), 1)
    upto = (src <= dst).astype(jnp.float32).astype(jnp.bfloat16)
    rank = jnp.dot(flags, upto, preferred_element_type=jnp.float32)[0:1, :].astype(jnp.int32)
    return jnp.where(on, rank, 0)


def project_kernel(chunk_start, own_ref, shard_ref, lab_hbm, seg_hbm, hid_hbm, w_hbm, mine_ref, theirs_ref, meta_ref, *rest):
    out_refs, (lab_ref, seg_ref, hid_ref, few_ref, acc_ref, small_sem, hid_sem, w_sem) = rest[:-8], rest[-8:]
    tokens, depth = hid_ref.shape
    rows = few_ref.shape[0]
    block = out_refs[0].shape[0]
    part = depth // hid_sem.shape[0]
    spans = [pl.ds(n, part) for n in range(0, depth, part)]
    count, chunk, _ = mine_ref.shape
    targets = [(theirs_ref, 1, n) for n in range(count)] + [(mine_ref, 0, n) for n in range(count)]
    starts = [chunk_start(shard_ref[0], slot, n) for _, slot, n in targets]
    small = [
        pltpu.make_async_copy(lab_hbm, lab_ref, small_sem.at[0]),
        pltpu.make_async_copy(seg_hbm, seg_ref, small_sem.at[1]),
    ]
    hid_copies = [
        pltpu.make_async_copy(hid_hbm.at[0, :, span], hid_ref.at[:, span], hid_sem.at[n])
        for n, span in enumerate(spans)
    ]
    w_copies = [
        pltpu.make_async_copy(w_hbm.at[0, pl.ds(start, chunk), :], ref.at[n], w_sem.at[m])
        for m, (start, (ref, _, n)) in enumerate(zip(starts, targets))
    ]
    queue = small + hid_copies + w_copies
    for copy in queue[: 2 + IN_FLIGHT]:
        copy.start()
    queue = queue[2 + IN_FLIGHT :]
    for copy in small:
        copy.wait()

    lab = lab_ref[...]
    seg = seg_ref[...]
    rank = ranks_along(lab)
    pick = rank == wanted_ranks(0, rows, own_ref[0], block)
    picker = pick.astype(jnp.float32).astype(jnp.bfloat16)
    for copy, span in zip(hid_copies, spans):
        copy.wait()
        if queue:
            queue.pop(0).start()
        few = jnp.dot(picker, hid_ref[:, span], preferred_element_type=jnp.float32)
        few_ref[:, span] = few.astype(jnp.bfloat16)

    mine = pick[:block, :]
    label = jnp.sum(jnp.where(mine, lab, 0).astype(jnp.float32), axis=1, keepdims=True)
    doc = jnp.sum(jnp.where(mine, seg, 0).astype(jnp.float32), axis=1, keepdims=True)
    same = (lab >= 0) & (seg.astype(jnp.float32) == doc)
    count = jnp.sum(jnp.where(same, 1.0, 0.0), axis=1, keepdims=True)
    weight = float(tokens) / (SEGS * jnp.maximum(count, 1.0))
    lane = lane_ids(block)
    meta_ref[...] = jnp.where(lane == 0, label, jnp.where(lane == 1, weight, 0.0))

    for m, (copy, start, (ref, _, n)) in enumerate(zip(w_copies, starts, targets)):
        copy.wait()
        if queue:
            queue.pop(0).start()
        term = jnp.dot(few_ref[:, pl.ds(start, chunk)], ref[n], preferred_element_type=jnp.float32)
        if m == 0:
            acc_ref[...] = term
        elif m < len(targets) - 1:
            acc_ref[...] += term
        else:
            logits = (acc_ref[...] + term).astype(jnp.bfloat16)
            for k, out_ref in enumerate(out_refs):
                out_ref[...] = logits[k * block : (k + 1) * block, :]


def project(ids, labels, segments, hidden, head_weight, peers, chunk_start, count):
    tokens, depth = hidden.shape[1:]
    width = head_weight.shape[2]
    rows = tokens - IGNORED
    block = rows // peers
    hbm = pl.BlockSpec(memory_space=pltpu.HBM)
    vmem = pl.BlockSpec(memory_space=pltpu.VMEM)
    return pl.pallas_call(
        functools.partial(project_kernel, chunk_start),
        in_specs=[pl.BlockSpec(memory_space=pltpu.SMEM)] * 2 + [hbm] * 4,
        out_specs=[vmem] * (3 + peers),
        out_shape=[jax.ShapeDtypeStruct((count, depth // (2 * count), width), jnp.bfloat16)] * 2
        + [jax.ShapeDtypeStruct((block, LANES), jnp.float32)]
        + [jax.ShapeDtypeStruct((block, width), jnp.bfloat16)] * peers,
        scratch_shapes=[
            pltpu.VMEM((1, tokens), jnp.int32),
            pltpu.VMEM((1, tokens), jnp.int32),
            pltpu.VMEM((tokens, depth), jnp.bfloat16),
            pltpu.VMEM((rows, depth), jnp.bfloat16),
            pltpu.VMEM((rows, width), jnp.float32),
            pltpu.SemaphoreType.DMA((2,)),
            pltpu.SemaphoreType.DMA((2,)),
            pltpu.SemaphoreType.DMA((2 * count,)),
        ],
        compiler_params=LARGE,
        cost_estimate=pl.CostEstimate(
            flops=2 * rows * depth * (width + tokens), bytes_accessed=0, transcendentals=0
        ),
        name="project",
    )(*ids, labels, segments, hidden, head_weight)


def pair_list(peers):
    return [(i, j) for i in range(peers) for j in range(peers) if i != j]


def stat_slots(peers):
    pairs = pair_list(peers)
    return peers, {p: peers + n for n, p in enumerate(pairs)}, peers + len(pairs)


def stats_kernel(own_ref, shard_ref, meta_ref, *refs):
    logit_refs, out_ref = refs[:-1], refs[-1]
    peers = len(logit_refs)
    block, width = logit_refs[0].shape
    _, pair_slot, target_slot = stat_slots(peers)
    span = LANES * GROUP // block
    lane = lane_ids(GROUP)
    sums = jnp.zeros((GROUP, LANES), jnp.float32)
    peaks = jnp.zeros((GROUP, LANES), jnp.float32)
    for g in range(block // GROUP):
        rows = slice(g * GROUP, (g + 1) * GROUP)
        label = meta_ref[rows, 0:1].astype(jnp.int32) - shard_ref[0] * width
        peak = []
        for ref in logit_refs:
            top = ref[rows, 0:LANES].astype(jnp.float32)
            for c in range(LANES, width, LANES):
                top = jnp.maximum(top, ref[rows, c : c + LANES].astype(jnp.float32))
            peak.append(jnp.max(top, axis=1, keepdims=True))
        total = [jnp.zeros((GROUP, LANES), jnp.float32) for _ in range(peers)]
        target = [jnp.zeros((GROUP, LANES), jnp.float32) for _ in range(peers)]
        cross = {p: jnp.zeros((GROUP, LANES), jnp.float32) for p in pair_slot}
        for c in range(0, width, LANES):
            l = [ref[rows, c : c + LANES].astype(jnp.float32) for ref in logit_refs]
            e = [jnp.exp(l[k] - peak[k]) for k in range(peers)]
            hit = (lane + c) == label
            for i in range(peers):
                total[i] += e[i]
                target[i] += jnp.where(hit, l[i], 0.0)
                for j in range(i + 1, peers):
                    gap = l[i] - l[j]
                    cross[i, j] += e[i] * gap
                    cross[j, i] -= e[j] * gap

        def put(slot, vals, top):
            nonlocal sums, peaks
            here = lane == g * span + slot
            sums = jnp.where(here, jnp.sum(vals, axis=1, keepdims=True), sums)
            if top is not None:
                peaks = jnp.where(here, top, peaks)

        for i in range(peers):
            put(i, total[i], peak[i])
            put(target_slot + i, target[i], None)
        for (i, j), slot in pair_slot.items():
            put(slot, cross[i, j], peak[i])
    out_ref[0:GROUP, :] = sums
    out_ref[GROUP : 2 * GROUP, :] = peaks


def stats(ids, meta, logits):
    block, width = logits[0].shape
    peers = len(logits)
    return pl.pallas_call(
        stats_kernel,
        in_specs=[pl.BlockSpec(memory_space=pltpu.SMEM)] * 2 + [pl.BlockSpec(memory_space=pltpu.VMEM)] * (1 + peers),
        out_shape=jax.ShapeDtypeStruct((2 * GROUP, LANES), jnp.float32),
        compiler_params=SMALL,
        cost_estimate=pl.CostEstimate(
            flops=40 * block * width * peers, bytes_accessed=2 * block * width * peers, transcendentals=block * width * peers
        ),
        name="stats",
    )(*ids, meta, *logits)


def merged(parts):
    top = parts[0][GROUP:, :]
    for part in parts[1:]:
        top = jnp.maximum(top, part[GROUP:, :])
    total = jnp.zeros_like(top)
    for part in parts:
        total += part[:GROUP, :] * jnp.exp(part[GROUP:, :] - top)
    return total, top


def merge_kernel(*refs):
    total, top = merged([ref[...] for ref in refs[:-1]])
    refs[-1][:GROUP, :] = total
    refs[-1][GROUP:, :] = top


def merge(parts):
    return pl.pallas_call(
        merge_kernel,
        in_specs=[pl.BlockSpec(memory_space=pltpu.VMEM)] * len(parts),
        out_shape=jax.ShapeDtypeStruct(parts[0].shape, jnp.float32),
        compiler_params=SMALL,
        name="merge",
    )(*parts)


def grad_kernel(count, own_ref, shard_ref, meta_ref, *refs):
    stat_refs, refs = refs[:count], refs[count:]
    peers = len(refs) // 3
    logit_refs, grad_refs, loss_refs = refs[:peers], refs[peers : 2 * peers], refs[2 * peers :]
    block, width = logit_refs[0].shape
    _, pair_slot, target_slot = stat_slots(peers)
    span = LANES * GROUP // block
    lane = lane_ids(GROUP)
    total, top = merged([ref[...] for ref in stat_refs])
    norm = top + jnp.log(jnp.maximum(total, 1e-37))
    third = 1.0 / (peers - 1)
    for g in range(block // GROUP):
        rows = slice(g * GROUP, (g + 1) * GROUP)
        at = lambda array, slot: array[:, g * span + slot : g * span + slot + 1]
        label = meta_ref[rows, 0:1].astype(jnp.int32) - shard_ref[0] * width
        weight = meta_ref[rows, 1:2]
        inverse = [1.0 / at(total, i) for i in range(peers)]
        norms = [at(norm, i) for i in range(peers)]
        mean = {p: at(total, slot) * inverse[p[0]] for p, slot in pair_slot.items()}
        shift = []
        for i in range(peers):
            ahead = sum(mean[i, j] for j in range(peers) if j != i)
            back = sum(mean[j, i] for j in range(peers) if j != i)
            loss = norms[i] - at(total, target_slot + i) + (ahead + back) * third
            loss_refs[i][rows, :] = jnp.broadcast_to(loss, (GROUP, LANES))
            shift.append(1.0 + (peers - ahead) * third)
        for c in range(0, width, LANES):
            l = [ref[rows, c : c + LANES].astype(jnp.float32) for ref in logit_refs]
            p = [jnp.exp(l[k] - norms[k]) for k in range(peers)]
            common = sum(l) * third
            rest = sum(p) * third + jnp.where((lane + c) == label, 1.0, 0.0)
            for i in range(peers):
                grad = p[i] * (shift[i] + (l[i] * (peers * third) - common)) - rest
                grad_refs[i][rows, c : c + LANES] = (weight * grad).astype(jnp.bfloat16)


def gradients(ids, meta, parts, logits):
    block, width = logits[0].shape
    peers = len(logits)
    return pl.pallas_call(
        functools.partial(grad_kernel, len(parts)),
        in_specs=[pl.BlockSpec(memory_space=pltpu.SMEM)] * 2
        + [pl.BlockSpec(memory_space=pltpu.VMEM)] * (1 + len(parts) + peers),
        out_shape=[jax.ShapeDtypeStruct((block, width), jnp.bfloat16)] * peers
        + [jax.ShapeDtypeStruct((block, LANES), jnp.float32)] * peers,
        compiler_params=SMALL,
        cost_estimate=pl.CostEstimate(
            flops=20 * block * width * peers, bytes_accessed=4 * block * width * peers, transcendentals=block * width * peers
        ),
        name="gradients",
    )(*ids, meta, *parts, *logits)


def share_of(w_ref, index, grad):
    return lax.dot_general(w_ref[index], grad, (((1,), (1,)), ((), ())), preferred_element_type=jnp.float32)


def both_shares(mask, shard_ref, refs):
    mine_ref, theirs_ref, own_ref, other_ref = refs
    index = (shard_ref[0] // 2) ^ mask
    return share_of(mine_ref, index, own_ref[...]) + share_of(theirs_ref, index, other_ref[...])


def gather_kernel(own_ref, shard_ref, *refs):
    block = refs[0].shape[0]
    for k, ref in enumerate(refs[:-1]):
        refs[-1][k * block : (k + 1) * block, :] = ref[...]


def vmem_call(kernel, outs, cost, name, ids, *arrays):
    return pl.pallas_call(
        kernel,
        in_specs=[pl.BlockSpec(memory_space=pltpu.SMEM)] * 2 + [pl.BlockSpec(memory_space=pltpu.VMEM)] * len(arrays),
        out_specs=[pl.BlockSpec(memory_space=pltpu.VMEM)] * len(outs),
        out_shape=[jax.ShapeDtypeStruct(shape, dtype) for shape, dtype in outs],
        compiler_params=SMALL,
        cost_estimate=cost,
        name=name,
    )(*ids, *arrays)


def coded(value):
    depth, rows = value.shape
    top = jnp.maximum(jnp.max(jnp.abs(value), axis=0, keepdims=True), 1e-30)
    code = jnp.ceil(jnp.log2(top) * CODE_STEPS)
    unit = jnp.exp2(code * (-1.0 / CODE_STEPS)) * CODE_TOP
    whole = jnp.clip(jnp.round(value * unit), -CODE_TOP - 1, CODE_TOP + 1)
    codes = jnp.broadcast_to(code, (CODE_ROWS, rows))
    return whole.astype(jnp.int32).astype(jnp.int16), codes.astype(jnp.int32).astype(jnp.int16)


def put_coded(ref, value):
    depth = value.shape[0]
    ref[:depth, :], ref[depth:, :] = coded(value)


def get_coded(ref):
    depth = ref.shape[0] - CODE_ROWS
    code = ref[depth:, :].astype(jnp.int32).astype(jnp.float32)[0:1, :]
    unit = jnp.exp2(code * (1.0 / CODE_STEPS)) * (1.0 / CODE_TOP)
    return ref[:depth, :].astype(jnp.int32).astype(jnp.float32) * unit


def encode_kernel(mask, own_ref, shard_ref, *refs):
    put_coded(refs[4], both_shares(mask, shard_ref, refs[:4]))


def is_middle(shard_ref):
    chip = shard_ref[0] // 2
    return (chip == 1) | (chip == 2)


def relay_kernel(own_ref, shard_ref, value_ref, coded_ref, out_ref):
    put_coded(out_ref, value_ref[...] + jnp.where(is_middle(shard_ref), get_coded(coded_ref), 0.0))


def own_sum_kernel(mask, own_ref, shard_ref, mine_ref, grad_ref, out_ref):
    out_ref[...] = share_of(mine_ref, (shard_ref[0] // 2) ^ mask, grad_ref[...])


def add_kernel(mask, own_ref, shard_ref, theirs_ref, grad_ref, part_ref, out_ref):
    put_coded(out_ref, part_ref[...] + share_of(theirs_ref, (shard_ref[0] // 2) ^ mask, grad_ref[...]))


def sum_kernel(mask, own_ref, shard_ref, *refs):
    refs[-1][...] = both_shares(mask, shard_ref, refs[:4])


def keep_kernel(own_ref, shard_ref, *refs):
    value = both_shares(0, shard_ref, refs[:4])
    for ref in refs[4:-1]:
        value += jnp.where(is_middle(shard_ref), 0.0, get_coded(ref))
    refs[-1][...] = value


def place_kernel(peers, own_ref, shard_ref, row_ref, *refs):
    loss_refs, (place_ref, out_ref) = refs[:peers], refs[peers:]
    tokens, rows = place_ref.shape
    block = rows // peers
    rank = ranks_along(row_ref[...])
    here = rank == wanted_ranks(0, rows, own_ref[0], block)
    out_ref[...] = jnp.sum(jnp.where(here, jnp.concatenate([ref[:, 0:1] for ref in loss_refs], axis=0), 0.0), axis=0, keepdims=True)

    src = lax.broadcasted_iota(jnp.int32, (tokens, tokens), 0)
    dst = lax.broadcasted_iota(jnp.int32, (tokens, tokens), 1)
    flags = (row_ref[...] >= 0).astype(jnp.float32).astype(jnp.bfloat16)
    flags = jnp.broadcast_to(flags, (LANES, tokens))
    turned = lambda keep: lax.dot_general(
        keep.astype(jnp.float32).astype(jnp.bfloat16),
        flags,
        (((1,), (1,)), ((), ())),
        preferred_element_type=jnp.float32,
    )[:, 0:1]
    rank = (turned(dst <= src) * turned(dst == src)).astype(jnp.int32)
    col = lax.broadcasted_iota(jnp.int32, (1, rows), 1)
    wanted = (own_ref[0] ^ (col // block)) * block + col % block + 1
    place_ref[...] = (rank == wanted).astype(jnp.float32).astype(jnp.bfloat16)


def place(ids, labels, losses, peers):
    tokens = labels.shape[1]
    return vmem_call(
        functools.partial(place_kernel, peers),
        [((tokens, tokens - IGNORED), jnp.bfloat16), ((1, tokens), jnp.float32)],
        pl.CostEstimate(flops=4 * tokens * tokens * LANES, bytes_accessed=0, transcendentals=0),
        "place",
        ids,
        labels,
        *losses,
    )


def finish_kernel(place_ref, sum_ref, *refs):
    coded_refs, (out_hbm, out_ref, sems) = refs[:-3], refs[-3:]
    value = sum_ref[...]
    for ref in coded_refs:
        value += get_coded(ref)
    high = value.astype(jnp.bfloat16)
    low = (value - high.astype(jnp.float32)).astype(jnp.bfloat16)
    turned = lambda place, piece: lax.dot_general(
        place, piece, (((1,), (1,)), ((), ())), preferred_element_type=jnp.float32
    )
    part = out_ref.shape[0] // sems.shape[0]
    copies = []
    for n in range(sems.shape[0]):
        span = pl.ds(n * part, part)
        place = place_ref[span, :]
        out_ref[span, :] = turned(place, high) + turned(place, low)
        copies.append(pltpu.make_async_copy(out_ref.at[span, :], out_hbm.at[0, span, :], sems.at[n]))
        copies[-1].start()
    for copy in copies:
        copy.wait()


def finish(placing, kept, arrived):
    tokens, rows = placing.shape
    depth = kept.shape[0]
    return pl.pallas_call(
        finish_kernel,
        in_specs=[pl.BlockSpec(memory_space=pltpu.VMEM)] * (2 + len(arrived)),
        out_specs=pl.BlockSpec(memory_space=pltpu.HBM),
        out_shape=jax.ShapeDtypeStruct((1, tokens, depth), jnp.float32),
        scratch_shapes=[pltpu.VMEM((tokens, depth), jnp.float32), pltpu.SemaphoreType.DMA((4,))],
        compiler_params=SMALL,
        cost_estimate=pl.CostEstimate(flops=1000, bytes_accessed=0, transcendentals=0),
        name="finish",
    )(placing, kept, *arrived)


def swap(array, axis, size, mask):
    return lax.ppermute(array, axis, [(i, i ^ mask) for i in range(size)])


def hop(array, pairs):
    return lax.ppermute(array, "vocab", [(2 * a + c, 2 * b + c) for a, b in pairs for c in range(2)])


def on_device(hidden, head_weight, labels, segments):
    peers = lax.axis_size("peer")
    shards = lax.axis_size("vocab")
    width = head_weight.shape[2]
    depth = head_weight.shape[1] // shards
    tokens = labels.shape[0]
    rows = tokens - IGNORED
    chips = shards // 2
    labels, segments = labels[None, :], segments[None, :]
    ids = [lax.axis_index(name).astype(jnp.int32).reshape(1) for name in ("peer", "vocab")]
    by_core = depth % LANES == 0

    def chunk_start(shard, slot, n):
        if by_core:
            return pl.multiple_of((2 * n + ((shard % 2) ^ slot)) * depth, depth)
        return (n + slot * PLAIN_CHUNKS) * (head_weight.shape[1] // (2 * PLAIN_CHUNKS))

    in_hbm = [pltpu.with_memory_space_constraint(x, pltpu.HBM) for x in (labels, segments, hidden, head_weight)]
    w_mine, w_theirs, meta, *blocks = project(
        ids, *in_hbm, peers, chunk_start, chips if by_core else PLAIN_CHUNKS
    )

    def across(arrays):
        moved = {k: swap(arrays[k], "peer", peers, k) for k in range(peers - 1, 0, -1)}
        return [arrays[0]] + [moved[k] for k in range(1, peers)]

    core_swap = lambda array: swap(array, "vocab", shards, 1)
    logits = across(blocks)
    part = stats(ids, meta, logits)
    part = merge([part, core_swap(part)])
    after = lambda array, *before: lax.optimization_barrier((array,) + before)[0]
    w_given = core_swap(after(w_theirs, part)) if by_core else None
    parts = [part] + [swap(part, "vocab", shards, 2 * mask) for mask in range(chips - 1, 0, -1)]
    outs = gradients(ids, meta, parts, logits)
    grads, losses = across(outs[:peers]), outs[peers:]

    cost = pl.CostEstimate(flops=1000, bytes_accessed=0, transcendentals=0)
    flat = ((rows, width), jnp.bfloat16)
    others = [core_swap(grad) for grad in grads]
    (own_grad,) = vmem_call(gather_kernel, [flat], cost, "gather", ids, *grads)
    (other_grad,) = vmem_call(gather_kernel, [flat], cost, "gather", ids, *others)
    if by_core:
        operands = (w_mine, w_given, own_grad, other_grad)
        coded_shape, full = ((depth + CODE_ROWS, rows), jnp.int16), ((depth, rows), jnp.float32)

        def encode(mask, *more):
            kernel = functools.partial(encode_kernel, mask)
            return vmem_call(kernel, [coded_shape, *more], cost, "encode", ids, *operands)

        if chips == 4:
            full = ((depth, rows), jnp.float32)
            kernel = functools.partial(own_sum_kernel, 2)
            (part,) = vmem_call(kernel, [full], cost, "share", ids, w_mine, own_grad)
            kernel = functools.partial(add_kernel, 2)
            (two,) = vmem_call(kernel, [coded_shape], cost, "encode", ids, w_given, other_grad, part)
            first = hop(two, [(0, 1), (3, 2), (1, 3), (2, 0)])
            kernel = functools.partial(sum_kernel, 3)
            (three,) = vmem_call(kernel, [full], cost, "share", ids, *operands)
            (one,) = encode(1)
            (relayed,) = vmem_call(relay_kernel, [coded_shape], cost, "relay", ids, three, first)
            cross = swap(relayed, "vocab", shards, 6)
            near = swap(one, "vocab", shards, 2)
            early, arrived = [first], [cross, near]
        else:
            early = []
            arrived = [swap(encode(mask)[0], "vocab", shards, 2 * mask) for mask in range(chips - 1, 0, -1)]
        (kept,) = vmem_call(keep_kernel, [((depth, rows), jnp.float32)], cost, "keep", ids, *operands, *early)
    else:
        arrived = []
        share = lax.dot_general(
            head_weight[0], own_grad, (((1,), (1,)), ((), ())), preferred_element_type=jnp.float32
        )
        kept = lax.psum_scatter(share, "vocab", scatter_dimension=0, tiled=True)
    losses = across([after(loss, kept) for loss in losses])
    placing, token_loss = place(ids, labels, losses, peers)
    grad_hidden = finish(placing, kept, arrived)
    return grad_hidden, token_loss


def solution(mesh):
    in_specs = (P("peer", None, None), P("peer", None, "vocab"), P(), P())
    out_specs = (P("peer", None, "vocab"), P("peer", None))
    return jax.shard_map(on_device, mesh=mesh, in_specs=in_specs, out_specs=out_specs, check_vma=False)
```
